32 devices in a mesh: grp: 2 (over y), tp: 4 (over z), req: 2 (over x), kv: 2 (over core).
Axes of the slice: x: 2, y: 2, z: 4, core: 2. Of those that a mesh axis runs over, the one named last changes fastest.
Arguments:
- tokens: bfloat16 [8, 128, 8192], P(('grp', 'req', 'kv'), 'tp'), parts along dimension 0, may hold values from -6 to 6
- norm_gain: bfloat16 [8192], replicated, may hold values from 0.3984375 to 1.59375
- w_query: bfloat16 [8192, 8192], P(('req', 'kv'), 'tp'), may hold values from -0.0625 to 0.0625
- w_key: bfloat16 [8192, 1024], P(('req', 'kv'), 'tp'), may hold values from -0.125 to 0.125
- w_value: bfloat16 [8192, 1024], P(('req', 'kv'), 'tp'), may hold values from -0.0625 to 0.0625
- w_out: bfloat16 [8192, 8192], P('tp', ('req', 'kv')), may hold values from -0.0625 to 0.0625
- cache_keys: bfloat16 [64, 64, 1024], P(('grp', 'req', 'kv')), parts along dimension 0, may hold values from -240 to 240
- cache_values: bfloat16 [64, 64, 1024], P(('grp', 'req', 'kv')), parts along dimension 0, may hold values from -6 to 6
- seg_ids: int32 [8, 128], P('grp'), parts along dimension 0, may hold values from 0 to 1, never falling along the last dimension, each value on 1 to 96 neighbouring positions
- block_ids: int32 [8, 2, 8], P('grp'), parts along dimension 0, may hold values from -1 to 31, as said below
Outputs:
- scored: bfloat16 [8, 128, 8192], P(('grp', 'req', 'kv'), 'tp'), parts along dimension 0
The draws below stay inside these ranges and needn't reach their ends.
There are 2 independent parts, one for each index of `grp`. The reference program is written for one: setup_inputs(seed, part) draws one part's arguments, and reference() takes and returns one part's arrays. A program takes and returns all parts, laid end to end along the dimension named above; an argument that names none is the same for every part. Nothing has to cross between parts.
Inputs may be any that keep to these rules, and one draw needn't show every extreme that they name: `block_ids`: slots 0 to 3 of every step hold blocks 0 to 3; the next slots hold the first 1 to 4 blocks of one branch l, ids 4 + l * 4 + j in order of j; the rest are -1. The first step of every group holds 8 blocks.
All inputs are finite; a program needn't handle non-finite values.
Results may differ from the reference program's by a relative error of at most 0.03.
Values may be sent and summed in bfloat16 or wider, within the bound.
No kernel may reach another device: no remote copies, remote signals or barrier semaphores. Data moves between devices by JAX's collectives and lax.ppermute only.
A program may use at most 192 MiB of HBM per device.

```python
import math
import jax
import jax.numpy as jnp
import numpy as np
from jax import lax

D = 8192
HQ = 64
KVH = 8
HD = 128
CR = 128
BLK = 64
STEPS = 2
ROOT = 4
CHAIN = 4
NRK = 4
NB = 32
LEAVES = 7
MAXB = 8
STEP_MAX = 96
N_TP = 4


def draw_cache_keys(key, part):
    key = jax.random.fold_in(key, 7)
    first = jax.random.fold_in(key, 0)
    base = jax.random.normal(first, (NB, BLK, KVH * HD), jnp.float32)
    return jnp.clip(base, -6.0, 6.0).astype(jnp.bfloat16)


def draw_block_ids(key, part):
    key = jax.random.fold_in(key, 5)
    first, second = jax.random.split(key)
    branch = jax.random.randint(first, (NRK, STEPS, 1), 0, LEAVES, jnp.int32)
    depth = jax.random.randint(second, (NRK, STEPS, 1), 1, CHAIN + 1, jnp.int32)
    depth = depth.at[:, 0].set(CHAIN)
    slots = jnp.arange(MAXB, dtype=jnp.int32)
    leaf_slot = slots - ROOT
    chosen = jnp.where(leaf_slot < depth, ROOT + branch * CHAIN + leaf_slot, -1)
    return jnp.where(slots < ROOT, slots, chosen).astype(jnp.int32)


def levels(rng, shape, pieces, least, top_value):
    level = 1.0
    for dim, parts in pieces:
        steps = jax.random.uniform(jax.random.fold_in(jax.random.fold_in(rng, 6), dim), (parts,), jnp.float32, least / len(pieces), top_value / len(pieces))
        level = level * jnp.repeat(jnp.exp(steps), shape[dim] // parts).reshape((-1,) + (1,) * (len(shape) - 1 - dim))
    return level


def split_up(count, total, reach, lean):
    loads = [(1 << 20) // math.isqrt(grade ** lean) + 1 for grade in range(2, count + 1)]
    rest, given = total - reach - (count - 1), [1] * (count - 1)
    while rest > 0:
        candidates = [i for i in range(count - 1) if given[i] < reach]
        mass, budget = sum([loads[i] for i in candidates]), rest
        for i in candidates:
            extra = min(reach - given[i], max(1, budget * loads[i] // mass), rest)
            given[i] = given[i] + extra
            rest = rest - extra
    return np.array([reach] + given)


def uneven(stream_key, count, total, reach, skew):
    if count == 2:
        one = jax.random.randint(stream_key, (), max(1, total - reach), min(reach, total - 1) + 1)
        return jnp.stack([one, total - one])
    lengths = jnp.asarray(split_up(count, total, reach, skew), jnp.int32)
    twos = (count - 1) // 2
    donor, sink = lengths[1:1 + 2 * twos:2], lengths[2:2 + 2 * twos:2]
    slack = jnp.minimum(donor - 1, reach - sink)
    passed = jax.random.randint(jax.random.fold_in(stream_key, 1), (twos,), 0, 1 << 20) % (slack + 1)
    lengths = lengths.at[1:1 + 2 * twos:2].set(donor - passed).at[2:2 + 2 * twos:2].set(sink + passed)
    return lengths[jax.random.permutation(jax.random.fold_in(stream_key, 2), count)]


def normal_values(own_key, dims, width, most, pieces=(), held_as=jnp.bfloat16):
    gain = levels(own_key, dims, pieces, -0.22, 0.18) if pieces else 1.0
    values = jax.random.normal(own_key, dims, jnp.float32) * width * gain
    return jnp.minimum(jnp.maximum(values, -most), most).astype(held_as)


def setup_inputs(seed: int = 0, part: int = 0) -> dict:
    streams_of = jax.random.split(jax.random.key(seed), 11)
    own_keys = jax.random.split(jax.random.fold_in(streams_of[10], part), 11)
    return {
        "tokens": normal_values(own_keys[0], (NRK, CR, D), 1.0, 6.0, ((0, 4), (1, 4))),
        "norm_gain": jnp.clip(1.0 + 0.12 * jax.random.normal(streams_of[1], (D,), jnp.float32), 0.3984375, 1.59375).astype(jnp.bfloat16),
        "w_query": normal_values(streams_of[2], (D, HQ * HD), D ** -0.5, 0.0625, ((0, 4), (1, 4))),
        "w_key": normal_values(streams_of[3], (D, KVH * HD), (D // 4) ** -0.5, 0.125, ((0, 4), (1, 4))),
        "w_value": normal_values(streams_of[4], (D, KVH * HD), D ** -0.5, 0.0625, ((0, 4), (1, 4))),
        "w_out": normal_values(streams_of[5], (HQ * HD, D), (HQ * HD) ** -0.5, 0.0625, ((0, 4), (1, 4))),
        "cache_keys": draw_cache_keys(jax.random.fold_in(jax.random.fold_in(streams_of[10], part), 71), part),
        "cache_values": normal_values(own_keys[7], (NB, BLK, KVH * HD), 1.0, 6.0, ((0, 4),)),
        "seg_ids": jax.vmap(lambda own: jnp.searchsorted(jnp.cumsum(uneven(own, STEPS, CR, STEP_MAX, 1)), jnp.arange(CR), side="right"))(jax.random.split(own_keys[8], NRK)).reshape((NRK, CR)).astype(jnp.int32),
        "block_ids": draw_block_ids(jax.random.fold_in(jax.random.fold_in(streams_of[10], part), 71), part),
    }


EPS = 1e-06

def reference(tokens, norm_gain, w_query, w_key, w_value, w_out, cache_keys, cache_values, seg_ids, block_ids):
    rows = tokens.shape[1]
    gsize = HQ // KVH
    member = jnp.any(block_ids[..., None] == jnp.arange(NB, dtype=jnp.int32), axis=-2)
    keys_all = cache_keys.astype(jnp.float32).reshape(NB * BLK, KVH, HD)
    values_all = cache_values.astype(jnp.float32).reshape(NB * BLK, KVH, HD)
    scale = HD ** (-0.5)

    def one_group(inputs):
        hidden, seg, mem = inputs
        wide = hidden.astype(jnp.float32)
        normed = (wide * lax.rsqrt(lax.optimization_barrier(jnp.mean(wide * wide, axis=-1, keepdims=True)) + EPS) * norm_gain.astype(jnp.float32)).astype(jnp.bfloat16)
        queries = jnp.dot(normed, w_query, preferred_element_type=jnp.float32).astype(jnp.bfloat16)
        new_keys = jnp.dot(normed, w_key, preferred_element_type=jnp.float32).astype(jnp.bfloat16)
        new_values = jnp.dot(normed, w_value, preferred_element_type=jnp.float32).astype(jnp.bfloat16)
        onehot = (seg[:, None] == jnp.arange(STEPS, dtype=jnp.int32)[None, :]).astype(jnp.float32)
        block_mask = jnp.dot(onehot, mem.astype(jnp.float32)) > 0.5
        cache_mask = jnp.repeat(block_mask, BLK, axis=1)
        places = jnp.arange(rows, dtype=jnp.int32)
        own_mask = (seg[:, None] == seg[None, :]) & (places[:, None] >= places[None, :])
        allowed = jnp.concatenate([cache_mask, own_mask], axis=1)
        keys = jnp.concatenate([keys_all, new_keys.astype(jnp.float32).reshape(rows, KVH, HD)], axis=0)
        values = jnp.concatenate([values_all, new_values.astype(jnp.float32).reshape(rows, KVH, HD)], axis=0)
        heads = queries.astype(jnp.float32).reshape(rows, KVH, gsize, HD)
        scores = jnp.einsum('rkgd,nkd->rkgn', heads, keys) * scale
        wide_mask = allowed[:, None, None, :]
        scores = jnp.where(wide_mask, scores, -1e+30)
        top = lax.optimization_barrier(jnp.max(scores, axis=-1, keepdims=True))
        weights = jnp.where(wide_mask, jnp.exp(scores - top), 0.0)
        total = lax.optimization_barrier(jnp.sum(weights, axis=-1))
        rounded = lax.optimization_barrier(weights.astype(jnp.bfloat16)).astype(jnp.float32)
        attended = (jnp.einsum('rkgn,nkd->rkgd', rounded, values) / total[..., None]).astype(jnp.bfloat16)
        attended = attended.reshape(rows, N_TP, HQ * HD // N_TP).transpose(1, 0, 2)
        out_sets = w_out.reshape(N_TP, HQ * HD // N_TP, D)

        def add_set(carry, pair):
            part_rows, part_weights = pair
            term = jnp.dot(part_rows, part_weights, preferred_element_type=jnp.float32)
            term = lax.optimization_barrier(term.astype(jnp.bfloat16)).astype(jnp.float32)
            return (carry + term, None)
        branch, unused = lax.scan(add_set, jnp.zeros((rows, D), jnp.float32), (attended, out_sets))
        return branch.astype(jnp.bfloat16)
    return lax.map(one_group, (tokens, seg_ids, member))
```

```python
import functools

import jax
import jax.numpy as jnp
from jax import lax
from jax.experimental import pallas as pl
from jax.experimental.pallas import tpu as pltpu
from jax.sharding import PartitionSpec as P

HQ = 64
KVH = 8
HD = 128


EPS = 1e-06


def swapped(block, axis, distance):
    count = lax.axis_size(axis)
    route = []
    for low in range(count):
        high = low | 1 << distance
        if high != low and high < count:
            route += [(low, high), (high, low)]
    return lax.ppermute(block, axis, route)


def combined_all(shard, axis, join):
    gathered = jax.tree.map(
        lambda a, kind: lax.all_gather(a.astype(kind), axis),
        shard,
        jax.tree.map(lambda a: jnp.bfloat16 if a.dtype == jnp.float32 else a.dtype, shard),
    )

    def take(source):
        return jax.tree.map(
            lambda a, own: lax.dynamic_index_in_dim(a, source, 0, False).astype(own.dtype),
            gathered,
            shard,
        )

    return lax.fori_loop(
        1, lax.axis_size(axis), lambda source, state: join(state, take(source)), take(0)
    )


def partial_attend(heads, keys, values, allowed, scale):
    scores = jnp.einsum("rkgd,nkd->rkgn", heads, keys, preferred_element_type=jnp.float32) * scale
    wide_mask = allowed[:, None, None, :]
    scores = jnp.where(wide_mask, scores, -1e30)
    top = jnp.max(scores, axis=-1)
    weights = jnp.where(wide_mask, jnp.exp(scores - top[..., None]), 0.0)
    total = jnp.sum(weights, axis=-1)
    summed = jnp.einsum(
        "rkgn,nkd->rkgd", weights.astype(jnp.bfloat16), values, preferred_element_type=jnp.float32
    )
    return (top, total, summed)


def combine(first, second):
    top = jnp.maximum(first[0], second[0])
    left = jnp.exp(first[0] - top)
    right = jnp.exp(second[0] - top)
    return (
        top,
        first[1] * left + second[1] * right,
        first[2] * left[..., None] + second[2] * right[..., None],
    )


def general_path(
    tokens, norm_gain, w_query, w_key, w_value, w_out, cache_keys, cache_values, seg_ids, block_ids
):
    groups = seg_ids.shape[0]
    rows = seg_ids.shape[1]
    steps = block_ids.shape[1]
    group = lax.axis_index(("req", "kv"))
    tp_index = lax.axis_index("tp")
    head_dim = HD
    gsize = HQ // KVH
    local_heads = w_query.shape[1] // head_dim
    per_kv = min(gsize, local_heads)
    kv_count = local_heads // per_kv
    first_kv = tp_index * local_heads // gsize
    scale = head_dim ** (-0.5)
    blocks_here = cache_keys.shape[0]
    block_len = cache_keys.shape[1]
    blocks_all = blocks_here * groups
    wide = tokens[0].astype(jnp.float32)
    normed = (
        wide
        * lax.rsqrt(jnp.mean(wide * wide, axis=-1, keepdims=True) + EPS)
        * norm_gain.astype(jnp.float32)
    ).astype(jnp.bfloat16)
    whole = lax.all_gather(normed, "tp", axis=0, tiled=True)
    pieces = (
        lax.all_gather(w_query, ("req", "kv"), axis=0, tiled=True),
        lax.all_gather(w_key, ("req", "kv"), axis=0, tiled=True),
        lax.all_gather(w_value, ("req", "kv"), axis=0, tiled=True),
    )
    query_acc, key_acc, value_acc = tuple(
        (jnp.dot(whole, piece, preferred_element_type=jnp.float32) for piece in pieces)
    )
    queries = query_acc.astype(jnp.bfloat16)
    span = max(1, gsize // local_heads)
    stacked = jnp.stack((key_acc.astype(jnp.bfloat16), value_acc.astype(jnp.bfloat16)))
    for bit in range(span.bit_length() - 1):
        partner = swapped(stacked, "tp", bit)
        upper = tp_index // (1 << bit) % 2 == 1
        stacked = jnp.where(
            upper, jnp.concatenate((partner, stacked), 2), jnp.concatenate((stacked, partner), 2)
        )
    own_keys = stacked[0].reshape(rows, kv_count, head_dim)
    own_values = stacked[1].reshape(rows, kv_count, head_dim)
    heads = queries.reshape(rows, kv_count, per_kv, head_dim)
    member = jnp.any(
        block_ids[..., None] == jnp.arange(blocks_all, dtype=jnp.int32), axis=-2
    ).astype(jnp.float32)
    onehot = (seg_ids[..., None] == jnp.arange(steps, dtype=jnp.int32)).astype(jnp.float32)
    block_mask = jnp.einsum("grs,gsb->grb", onehot, member) > 0.5
    seg_here = lax.dynamic_index_in_dim(seg_ids, group, 0, keepdims=False)
    places = jnp.arange(rows, dtype=jnp.int32)
    own_mask = (seg_here[:, None] == seg_here[None, :]) & (places[:, None] >= places[None, :])
    own_part = partial_attend(heads, own_keys, own_values, own_mask, scale)
    gathered = lax.all_gather(queries[None], ("req", "kv"), axis=0, tiled=True)
    all_heads = gathered.reshape(groups * rows, kv_count, per_kv, head_dim)
    local_keys = lax.dynamic_slice_in_dim(
        cache_keys, first_kv * head_dim, kv_count * head_dim, 2
    ).reshape(blocks_here * block_len, kv_count, head_dim)
    local_values = lax.dynamic_slice_in_dim(
        cache_values, first_kv * head_dim, kv_count * head_dim, 2
    ).reshape(blocks_here * block_len, kv_count, head_dim)
    local_blocks = lax.dynamic_slice_in_dim(
        block_mask, group * blocks_here, blocks_here, 2
    ).reshape(groups * rows, blocks_here)
    local_mask = jnp.repeat(local_blocks, block_len, axis=1)
    cache_part = partial_attend(all_heads, local_keys, local_values, local_mask, scale)
    merged = combined_all(cache_part, ("req", "kv"), combine)
    mine = tuple((lax.dynamic_slice_in_dim(item, group * rows, rows, 0) for item in merged))
    top, total, summed = combine(mine, own_part)
    attended = (
        (summed / total[..., None]).astype(jnp.bfloat16).reshape(rows, local_heads * head_dim)
    )
    out_full = lax.all_gather(w_out, ("req", "kv"), axis=1, tiled=True)
    branch = lax.psum_scatter(
        jnp.dot(attended, out_full, preferred_element_type=jnp.float32).astype(jnp.bfloat16),
        "tp",
        scatter_dimension=0,
        tiled=True,
    )
    return branch[None]


SWAP = [(0, 1), (1, 0)]
MASKED = -1e30


def tp_ring(count):
    return list(range(0, count, 2)) + list(range(1, count, 2))[::-1]


def picked(index, options):
    result = options[0]
    for number, option in enumerate(options[1:], 1):
        result = jnp.where(index == number, option, result)
    return result


def project_kernel(half_ref, x_ref, q_ref, k_ref, v_ref, out_ref):
    tile = pl.program_id(0)
    last = pl.num_programs(0) - 1
    width = q_ref.shape[1]
    head_dim = k_ref.shape[1]
    x = x_ref[...]

    @pl.when(tile < last)
    def _():
        product = jnp.dot(x, q_ref[...], preferred_element_type=jnp.float32)
        at = pl.multiple_of(tile * width, width)
        out_ref[:, pl.ds(at, width)] = product.astype(out_ref.dtype)

    @pl.when(tile == last)
    def _():
        base = last * width
        for number, ref in enumerate((k_ref, v_ref)):
            product = jnp.dot(x, ref[...], preferred_element_type=jnp.float32)
            at = base + number * head_dim
            out_ref[:, at : at + head_dim] = product.astype(out_ref.dtype)


def project(x, w_query, w_key, w_value, half, kind):
    rows, depth = x.shape
    q_cols = w_query.shape[1] // 2
    kv_cols = w_key.shape[1] // 2
    width = 256
    tiles = q_cols // width
    total = q_cols + 2 * kv_cols
    grid_spec = pltpu.PrefetchScalarGridSpec(
        num_scalar_prefetch=1,
        grid=(tiles + 1,),
        in_specs=[
            pl.BlockSpec((rows, depth), lambda t, h: (0, 0)),
            pl.BlockSpec(
                (depth, width), lambda t, h: (0, h[0] * tiles + jnp.minimum(t, tiles - 1))
            ),
            pl.BlockSpec((depth, kv_cols), lambda t, h: (0, h[0])),
            pl.BlockSpec((depth, kv_cols), lambda t, h: (0, h[0])),
        ],
        out_specs=pl.BlockSpec((rows, total), lambda t, h: (0, 0)),
    )
    return pl.pallas_call(
        project_kernel,
        grid_spec=grid_spec,
        out_shape=jax.ShapeDtypeStruct((rows, total), kind),
        compiler_params=pltpu.CompilerParams(vmem_limit_bytes=32 * 2**20),
        cost_estimate=pl.CostEstimate(
            flops=2 * rows * depth * total,
            bytes_accessed=2 * depth * total + 2 * rows * depth + 4 * rows * total,
            transcendentals=0,
        ),
        name="project",
    )(half, x, w_query, w_key, w_value)


def out_kernel(half_ref, own_ref, other_ref, w_ref, out_ref):
    depth = own_ref.shape[1]
    mine = half_ref[0]
    at = pl.multiple_of(mine * depth, depth)
    off = pl.multiple_of((1 - mine) * depth, depth)
    product = jnp.dot(own_ref[...], w_ref[pl.ds(at, depth), :], preferred_element_type=jnp.float32)
    product += jnp.dot(
        other_ref[...], w_ref[pl.ds(off, depth), :], preferred_element_type=jnp.float32
    )
    out_ref[...] = product.astype(out_ref.dtype)


def out_project(own, other, w_out, half):
    rows, depth = own.shape
    columns = w_out.shape[1]
    width = 256
    grid_spec = pltpu.PrefetchScalarGridSpec(
        num_scalar_prefetch=1,
        grid=(columns // width,),
        in_specs=[
            pl.BlockSpec((rows, depth), lambda t, h: (0, 0)),
            pl.BlockSpec((rows, depth), lambda t, h: (0, 0)),
            pl.BlockSpec((2 * depth, width), lambda t, h: (0, t)),
        ],
        out_specs=pl.BlockSpec((rows, width), lambda t, h: (0, t)),
    )
    return pl.pallas_call(
        out_kernel,
        grid_spec=grid_spec,
        out_shape=jax.ShapeDtypeStruct((rows, columns), jnp.bfloat16),
        compiler_params=pltpu.CompilerParams(vmem_limit_bytes=32 * 2**20),
        cost_estimate=pl.CostEstimate(
            flops=4 * rows * depth * columns,
            bytes_accessed=4 * depth * columns + 4 * rows * depth + 2 * rows * columns,
            transcendentals=0,
        ),
        name="out_project",
    )(half, own, other, w_out)


def attend_kernel(
    pieces, groups, steps, info_ref, keep_ref, come_ref, ck_ref, cv_ref, out_ref
):
    rows_all, total_cols = keep_ref.shape
    part = rows_all // (pieces * groups)
    rows = part * pieces
    head_dim = ck_ref.shape[1]
    heads = total_cols // head_dim - 2
    scale = head_dim**-0.5
    place = lax.broadcasted_iota(jnp.int32, (rows, rows), 0)
    across = lax.broadcasted_iota(jnp.int32, (rows, rows), 1)

    def position(index):
        piece = index // part
        start = jnp.full(index.shape, info_ref[0], jnp.int32)
        for j in range(1, pieces):
            start = jnp.where(piece == j, info_ref[j], start)
        return start * part + index % part

    row_pos = position(place)
    col_pos = position(across)
    own_rows = []
    for g in range(groups):
        own_rows.append(
            jnp.concatenate(
                [
                    (
                        keep_ref[(j * groups + g) * part : (j * groups + g + 1) * part, :]
                        + come_ref[(j * groups + g) * part : (j * groups + g + 1) * part, :].astype(
                            jnp.float32
                        )
                    ).astype(jnp.bfloat16)
                    for j in range(pieces)
                ],
                axis=0,
            )
        )
    for g in range(groups):
        qkv = own_rows[g]
        q_cols = heads * head_dim
        keys = [ck_ref[0:ROOT_KEYS, :]]
        values = [cv_ref[0:ROOT_KEYS, :]]
        bias = [jnp.zeros((rows, ROOT_KEYS), jnp.float32)]
        same = None
        for s in range(steps):
            at = pieces + (g * steps + s) * 4
            start, count = info_ref[at], info_ref[at + 1]
            low, high = info_ref[at + 2], info_ref[at + 3]
            begin = pl.multiple_of(start, CHAIN_KEYS)
            keys.append(ck_ref[pl.ds(begin, CHAIN_KEYS), :])
            values.append(cv_ref[pl.ds(begin, CHAIN_KEYS), :])
            row_in = (row_pos >= low) & (row_pos < high)
            col_in = (col_pos >= low) & (col_pos < high)
            both = row_in & col_in
            same = both if same is None else same | both
            for piece in range(CHAIN_KEYS // rows):
                allowed = row_in & (across + piece * rows < count)
                bias.append(jnp.where(allowed, 0.0, MASKED))
        keys.append(qkv[:, q_cols : q_cols + head_dim])
        values.append(qkv[:, q_cols + head_dim :])
        bias.append(jnp.where(same & (col_pos <= row_pos), 0.0, MASKED))
        keys = jnp.concatenate(keys, axis=0)
        values = jnp.concatenate(values, axis=0)
        bias = jnp.concatenate(bias, axis=1)
        for h in range(heads):
            query = qkv[:, h * head_dim : (h + 1) * head_dim]
            scores = lax.dot_general(
                query, keys, (((1,), (1,)), ((), ())), preferred_element_type=jnp.float32
            )
            scores = scores * scale + bias
            top = jnp.max(scores, axis=1, keepdims=True)
            weights = jnp.exp(scores - top)
            total = jnp.sum(weights, axis=1, keepdims=True)
            summed = jnp.dot(
                weights.astype(jnp.bfloat16), values, preferred_element_type=jnp.float32
            )
            result = (summed / total).astype(out_ref.dtype)
            for j in range(pieces):
                to = (j * groups + g) * part
                out_ref[to : to + part, h * head_dim : (h + 1) * head_dim] = result[
                    j * part : (j + 1) * part
                ]


def attend(keep, come, cache_k, cache_v, info, pieces, groups, steps):
    rows, total = keep.shape
    head_dim = cache_k.shape[1]
    heads = total // head_dim - 2
    per_group = rows // groups
    keys = ROOT_KEYS + steps * CHAIN_KEYS + per_group
    whole = pl.BlockSpec(memory_space=pltpu.VMEM)
    return pl.pallas_call(
        functools.partial(attend_kernel, pieces, groups, steps),
        in_specs=[pl.BlockSpec(memory_space=pltpu.SMEM)] + [whole] * 4,
        out_specs=whole,
        out_shape=jax.ShapeDtypeStruct((rows, heads * head_dim), jnp.bfloat16),
        compiler_params=pltpu.CompilerParams(vmem_limit_bytes=32 * 2**20),
        cost_estimate=pl.CostEstimate(
            flops=4 * rows * heads * keys * head_dim,
            bytes_accessed=4 * cache_k.size + 6 * rows * total,
            transcendentals=rows * heads * keys,
        ),
        name="attend",
    )(info, keep, come, cache_k, cache_v)


ROOT_BLOCKS = 4
CHAIN_BLOCKS = 4
BLOCK_KEYS = 64
ROOT_KEYS = ROOT_BLOCKS * BLOCK_KEYS
CHAIN_KEYS = CHAIN_BLOCKS * BLOCK_KEYS


def on_device(
    tokens, norm_gain, w_query, w_key, w_value, w_out, cache_keys, cache_values, seg_ids, block_ids
):
    req, kv, tp = lax.axis_index("req"), lax.axis_index("kv"), lax.axis_index("tp")
    cores = 2
    head_dim = HD
    steps = block_ids.shape[1]
    depth = w_query.shape[0]
    part = tokens.shape[1]
    blocks_here = cache_keys.shape[0]
    count = lax.axis_size("tp")
    order = tp_ring(count)
    forward = [(order[i], order[(i + 1) % count]) for i in range(count)]
    half = kv.astype(jnp.int32).reshape(1)
    other = (1 - kv).astype(jnp.int32).reshape(1)

    def swap_req(x):
        return lax.ppermute(x, "req", SWAP)

    def swap_kv(x):
        return lax.ppermute(x, "kv", SWAP)

    def onward(x):
        return lax.ppermute(x, "tp", forward)

    wide = tokens[0].astype(jnp.float32)
    normed = (
        wide
        * lax.rsqrt(jnp.mean(wide * wide, axis=-1, keepdims=True) + EPS)
        * norm_gain.astype(jnp.float32)
    ).astype(jnp.bfloat16)
    quarters = normed.reshape(part, 2, cores, depth)
    kept = lax.dynamic_index_in_dim(quarters, kv, 2, False)
    came = swap_kv(lax.dynamic_index_in_dim(quarters, 1 - kv, 2, False))
    both = jnp.where(kv == 0, jnp.stack((kept, came)), jnp.stack((came, kept)))
    near = lax.dynamic_index_in_dim(both, req, 2, False).reshape(cores * part, depth)
    far = swap_req(
        lax.dynamic_index_in_dim(both, 1 - req, 2, False).reshape(cores * part, depth)
    )

    def own_head(cache):
        local = 2 * head_dim * tp
        mine = lax.dynamic_slice_in_dim(cache, local + kv * head_dim, head_dim, 2)
        give = lax.dynamic_slice_in_dim(cache, local + (1 - kv) * head_dim, head_dim, 2)
        return mine, give

    k_mine, k_give = own_head(cache_keys)
    v_mine, v_give = own_head(cache_values)
    c_mine = jnp.stack((k_mine, v_mine))
    c_come = swap_kv(jnp.stack((k_give, v_give)))
    chip = jnp.where(
        kv == 0, jnp.stack((c_mine, c_come), 1), jnp.stack((c_come, c_mine), 1)
    )
    chip_far = swap_req(chip)
    cached = jnp.where(req == 0, jnp.stack((chip, chip_far), 1), jnp.stack((chip_far, chip), 1))
    cached = cached.reshape(2, 4 * blocks_here * BLOCK_KEYS, head_dim)

    seg_near = lax.dynamic_slice_in_dim(seg_ids, req * cores, cores, 0)
    ids_near = lax.dynamic_slice_in_dim(block_ids, req * cores, cores, 0)
    here = jnp.arange(steps, dtype=jnp.int32)
    low = jnp.sum(seg_near[:, None, :] < here[:, None], axis=-1, dtype=jnp.int32)
    high = jnp.sum(seg_near[:, None, :] <= here[:, None], axis=-1, dtype=jnp.int32)
    begin = ids_near[:, :, ROOT_BLOCKS] * BLOCK_KEYS
    length = jnp.sum(ids_near[:, :, ROOT_BLOCKS:] >= 0, axis=-1, dtype=jnp.int32) * BLOCK_KEYS
    spot = picked(tp, [order.index(i) for i in range(count)])
    sources = [
        picked((spot - j) % count, [jnp.int32(i) for i in order]) for j in range(count)
    ]
    info = jnp.concatenate(
        (
            jnp.stack(sources).astype(jnp.int32),
            jnp.stack((begin, length, low, high), axis=-1).reshape(-1).astype(jnp.int32),
        )
    )

    near_pieces, far_pieces = [near], [far]
    for _ in range(count - 1):
        near_pieces.append(onward(near_pieces[-1]))
        far_pieces.append(onward(far_pieces[-1]))
    far_rows = jnp.concatenate(far_pieces)
    near_rows = jnp.concatenate(near_pieces)
    weights = (w_query, w_key, w_value)
    far_sent = swap_kv(project(far_rows, *weights, other, jnp.bfloat16))
    far_kept = project(far_rows, *weights, half, jnp.float32)
    come = swap_req((far_kept + far_sent.astype(jnp.float32)).astype(jnp.bfloat16))
    near_sent = swap_kv(project(near_rows, *weights, other, jnp.bfloat16))
    near_kept = project(near_rows, *weights, half, jnp.float32)
    keep = near_kept + near_sent.astype(jnp.float32)

    attended = attend(keep, come, cached[0], cached[1], info, count, cores, steps)

    attended_far = swap_req(attended)
    near_sum = out_project(attended, swap_kv(attended), w_out, half)
    far_sum = out_project(attended_far, swap_kv(attended_far), w_out, half)

    def summed(terms):
        size = cores * part
        chunk = [terms[j * size : (j + 1) * size] for j in range(count)]
        running = onward(chunk[1])
        for j in range(2, count):
            running = onward(
                (running.astype(jnp.float32) + chunk[j].astype(jnp.float32)).astype(jnp.bfloat16)
            )
        return (running.astype(jnp.float32) + chunk[0].astype(jnp.float32)).astype(jnp.bfloat16)

    near_out = summed(near_sum)
    far_out = swap_req(summed(far_sum))
    columns = near_out.shape[1]
    outs = jnp.stack(
        (near_out.reshape(cores, part, columns), far_out.reshape(cores, part, columns)), 2
    )
    mine = lax.dynamic_index_in_dim(outs, kv, 0, False)
    come_out = swap_kv(lax.dynamic_index_in_dim(outs, 1 - kv, 0, False))
    chip_out = jnp.where(kv == 0, jnp.stack((mine, come_out), 2), jnp.stack((come_out, mine), 2))
    scored = jnp.where(req == 0, chip_out, chip_out[:, ::-1])
    return scored.reshape(1, part, 4 * columns)


def fits(shape, args):
    local_kv = KVH // shape["tp"]
    return shape["req"] == 2 and shape["kv"] == 2 and shape["tp"] > 1 and local_kv == 2


def solution(mesh):
    placed = (
        P(("grp", "req", "kv"), "tp", None),
        P(),
        P(("req", "kv"), "tp"),
        P(("req", "kv"), "tp"),
        P(("req", "kv"), "tp"),
        P("tp", ("req", "kv")),
        P(("grp", "req", "kv"), None, None),
        P(("grp", "req", "kv"), None, None),
        P("grp", None),
        P("grp", None, None),
    )
    return jax.shard_map(
        on_device if fits(mesh.shape, None) else general_path,
        mesh=mesh,
        in_specs=placed,
        out_specs=P(("grp", "req", "kv"), "tp", None),
        check_vma=False,
    )
```

```python
import functools

import jax
import jax.numpy as jnp
from jax import lax
from jax.experimental import pallas as pl
from jax.experimental.pallas import tpu as pltpu
from jax.sharding import PartitionSpec as P

HQ = 64
KVH = 8
HD = 128


EPS = 1e-06


def swapped(block, axis, distance):
    count = lax.axis_size(axis)
    route = []
    for low in range(count):
        high = low | 1 << distance
        if high != low and high < count:
            route += [(low, high), (high, low)]
    return lax.ppermute(block, axis, route)


def combined_all(shard, axis, join):
    gathered = jax.tree.map(
        lambda a, kind: lax.all_gather(a.astype(kind), axis),
        shard,
        jax.tree.map(lambda a: jnp.bfloat16 if a.dtype == jnp.float32 else a.dtype, shard),
    )

    def take(source):
        return jax.tree.map(
            lambda a, own: lax.dynamic_index_in_dim(a, source, 0, False).astype(own.dtype),
            gathered,
            shard,
        )

    return lax.fori_loop(
        1, lax.axis_size(axis), lambda source, state: join(state, take(source)), take(0)
    )


def partial_attend(heads, keys, values, allowed, scale):
    scores = jnp.einsum("rkgd,nkd->rkgn", heads, keys, preferred_element_type=jnp.float32) * scale
    wide_mask = allowed[:, None, None, :]
    scores = jnp.where(wide_mask, scores, -1e30)
    top = jnp.max(scores, axis=-1)
    weights = jnp.where(wide_mask, jnp.exp(scores - top[..., None]), 0.0)
    total = jnp.sum(weights, axis=-1)
    summed = jnp.einsum(
        "rkgn,nkd->rkgd", weights.astype(jnp.bfloat16), values, preferred_element_type=jnp.float32
    )
    return (top, total, summed)


def combine(first, second):
    top = jnp.maximum(first[0], second[0])
    left = jnp.exp(first[0] - top)
    right = jnp.exp(second[0] - top)
    return (
        top,
        first[1] * left + second[1] * right,
        first[2] * left[..., None] + second[2] * right[..., None],
    )


def general_path(
    tokens, norm_gain, w_query, w_key, w_value, w_out, cache_keys, cache_values, seg_ids, block_ids
):
    groups = seg_ids.shape[0]
    rows = seg_ids.shape[1]
    steps = block_ids.shape[1]
    group = lax.axis_index(("req", "kv"))
    tp_index = lax.axis_index("tp")
    head_dim = HD
    gsize = HQ // KVH
    local_heads = w_query.shape[1] // head_dim
    per_kv = min(gsize, local_heads)
    kv_count = local_heads // per_kv
    first_kv = tp_index * local_heads // gsize
    scale = head_dim ** (-0.5)
    blocks_here = cache_keys.shape[0]
    block_len = cache_keys.shape[1]
    blocks_all = blocks_here * groups
    wide = tokens[0].astype(jnp.float32)
    normed = (
        wide
        * lax.rsqrt(jnp.mean(wide * wide, axis=-1, keepdims=True) + EPS)
        * norm_gain.astype(jnp.float32)
    ).astype(jnp.bfloat16)
    whole = lax.all_gather(normed, "tp", axis=0, tiled=True)
    pieces = (
        lax.all_gather(w_query, ("req", "kv"), axis=0, tiled=True),
        lax.all_gather(w_key, ("req", "kv"), axis=0, tiled=True),
        lax.all_gather(w_value, ("req", "kv"), axis=0, tiled=True),
    )
    query_acc, key_acc, value_acc = tuple(
        (jnp.dot(whole, piece, preferred_element_type=jnp.float32) for piece in pieces)
    )
    queries = query_acc.astype(jnp.bfloat16)
    span = max(1, gsize // local_heads)
    stacked = jnp.stack((key_acc.astype(jnp.bfloat16), value_acc.astype(jnp.bfloat16)))
    for bit in range(span.bit_length() - 1):
        partner = swapped(stacked, "tp", bit)
        upper = tp_index // (1 << bit) % 2 == 1
        stacked = jnp.where(
            upper, jnp.concatenate((partner, stacked), 2), jnp.concatenate((stacked, partner), 2)
        )
    own_keys = stacked[0].reshape(rows, kv_count, head_dim)
    own_values = stacked[1].reshape(rows, kv_count, head_dim)
    heads = queries.reshape(rows, kv_count, per_kv, head_dim)
    member = jnp.any(
        block_ids[..., None] == jnp.arange(blocks_all, dtype=jnp.int32), axis=-2
    ).astype(jnp.float32)
    onehot = (seg_ids[..., None] == jnp.arange(steps, dtype=jnp.int32)).astype(jnp.float32)
    block_mask = jnp.einsum("grs,gsb->grb", onehot, member) > 0.5
    seg_here = lax.dynamic_index_in_dim(seg_ids, group, 0, keepdims=False)
    places = jnp.arange(rows, dtype=jnp.int32)
    own_mask = (seg_here[:, None] == seg_here[None, :]) & (places[:, None] >= places[None, :])
    own_part = partial_attend(heads, own_keys, own_values, own_mask, scale)
    gathered = lax.all_gather(queries[None], ("req", "kv"), axis=0, tiled=True)
    all_heads = gathered.reshape(groups * rows, kv_count, per_kv, head_dim)
    local_keys = lax.dynamic_slice_in_dim(
        cache_keys, first_kv * head_dim, kv_count * head_dim, 2
    ).reshape(blocks_here * block_len, kv_count, head_dim)
    local_values = lax.dynamic_slice_in_dim(
        cache_values, first_kv * head_dim, kv_count * head_dim, 2
    ).reshape(blocks_here * block_len, kv_count, head_dim)
    local_blocks = lax.dynamic_slice_in_dim(
        block_mask, group * blocks_here, blocks_here, 2
    ).reshape(groups * rows, blocks_here)
    local_mask = jnp.repeat(local_blocks, block_len, axis=1)
    cache_part = partial_attend(all_heads, local_keys, local_values, local_mask, scale)
    merged = combined_all(cache_part, ("req", "kv"), combine)
    mine = tuple((lax.dynamic_slice_in_dim(item, group * rows, rows, 0) for item in merged))
    top, total, summed = combine(mine, own_part)
    attended = (
        (summed / total[..., None]).astype(jnp.bfloat16).reshape(rows, local_heads * head_dim)
    )
    out_full = lax.all_gather(w_out, ("req", "kv"), axis=1, tiled=True)
    branch = lax.psum_scatter(
        jnp.dot(attended, out_full, preferred_element_type=jnp.float32).astype(jnp.bfloat16),
        "tp",
        scatter_dimension=0,
        tiled=True,
    )
    return branch[None]


SWAP = [(0, 1), (1, 0)]
MASKED = -1e30
MIB = 2**20


def tp_ring(count):
    return list(range(0, count, 2)) + list(range(1, count, 2))[::-1]


def after(value, *gates):
    if not gates:
        return value
    return lax.optimization_barrier((value, gates))[0]


def norm_kernel(place_ref, x_ref, gain_ref, keep_ref, give_ref, far_ref, cross_ref):
    wide = x_ref[0].astype(jnp.float32)
    factor = lax.rsqrt(jnp.mean(wide * wide, axis=1, keepdims=True) + EPS)
    width = keep_ref.shape[1]
    req, kv = place_ref[0], place_ref[1]
    to = (2 * req + kv, 2 * req + 1 - kv, 2 - 2 * req + kv, 3 - 2 * req - kv)
    for quarter, ref in zip(to, (keep_ref, give_ref, far_ref, cross_ref)):
        at = pl.multiple_of(quarter * width, width)
        part = x_ref[0, :, pl.ds(at, width)].astype(jnp.float32)
        gain = gain_ref[:, pl.ds(at, width)].astype(jnp.float32)
        ref[...] = (part * factor * gain).astype(ref.dtype)


def norm(place, tokens, gain):
    rows, depth = tokens.shape[1:]
    whole = pl.BlockSpec(memory_space=pltpu.VMEM)
    quarter = jax.ShapeDtypeStruct((rows, depth // 4), jnp.bfloat16)
    return pl.pallas_call(
        norm_kernel,
        in_specs=[pl.BlockSpec(memory_space=pltpu.SMEM), whole, whole],
        out_specs=[whole] * 4,
        out_shape=[quarter] * 4,
        compiler_params=pltpu.CompilerParams(vmem_limit_bytes=4 * MIB),
        name="norm",
    )(place, tokens, gain.reshape(1, depth))


def load_kernel(count, *refs):
    copies = [
        pltpu.make_async_copy(source, to, refs[-1].at[number])
        for number, (source, to) in enumerate(zip(refs[:count], refs[count:]))
    ]
    for copy in copies:
        copy.start()
    for copy in copies:
        copy.wait()


def load(limit, *arrays):
    count = len(arrays)
    return pl.pallas_call(
        functools.partial(load_kernel, count),
        in_specs=[pl.BlockSpec(memory_space=pl.ANY)] * count,
        out_specs=[pl.BlockSpec(memory_space=pltpu.VMEM)] * count,
        out_shape=[pltpu.VMEM(a.shape, a.dtype) for a in arrays],
        scratch_shapes=[pltpu.SemaphoreType.DMA((count,))],
        compiler_params=pltpu.CompilerParams(vmem_limit_bytes=limit * MIB),
        name="load",
    )(*arrays)


def heads_kernel(place_ref, k_ref, v_ref, mine_ref, give_ref, sems):
    head_dim = mine_ref.shape[-1]
    kv, tp = place_ref[1], place_ref[2]
    copies = []
    for number, (out, core) in enumerate(((mine_ref, kv), (give_ref, 1 - kv))):
        at = pl.multiple_of((2 * tp + core) * head_dim, head_dim)
        for which, ref in enumerate((k_ref, v_ref)):
            copies.append(
                pltpu.make_async_copy(
                    ref.at[:, :, pl.ds(at, head_dim)], out.at[which], sems.at[2 * number + which]
                )
            )
    for copy in copies:
        copy.start()
    for copy in copies:
        copy.wait()


def cached_heads(place, keys, values):
    blocks, length = keys.shape[:2]
    out = jax.ShapeDtypeStruct((2, blocks, length, HD), keys.dtype)
    return pl.pallas_call(
        heads_kernel,
        in_specs=[pl.BlockSpec(memory_space=pltpu.SMEM)]
        + [pl.BlockSpec(memory_space=pl.ANY)] * 2,
        out_specs=[pl.BlockSpec(memory_space=pltpu.VMEM)] * 2,
        out_shape=[out] * 2,
        scratch_shapes=[pltpu.SemaphoreType.DMA((4,))],
        compiler_params=pltpu.CompilerParams(vmem_limit_bytes=4 * MIB),
        name="cached_heads",
    )(place, keys, values)


def merge_kernel(place_ref, mine_ref, theirs_ref, out_ref):
    rows = mine_ref.shape[0]
    kv = place_ref[1]
    out_ref[pl.ds(pl.multiple_of(kv * rows, rows), rows), :] = mine_ref[...]
    out_ref[pl.ds(pl.multiple_of((1 - kv) * rows, rows), rows), :] = theirs_ref[...]


def merge(place, mine, theirs):
    rows, columns = mine.shape
    whole = pl.BlockSpec(memory_space=pltpu.VMEM)
    return pl.pallas_call(
        merge_kernel,
        in_specs=[pl.BlockSpec(memory_space=pltpu.SMEM)] + [whole] * 2,
        out_specs=whole,
        out_shape=jax.ShapeDtypeStruct((2 * rows, columns), mine.dtype),
        compiler_params=pltpu.CompilerParams(vmem_limit_bytes=4 * MIB),
        name="merge",
    )(place, mine, theirs)


def share_kernel(place_ref, running_ref, term_ref, mine_ref, give_ref):
    rows = mine_ref.shape[0]
    kv = place_ref[1]
    for core, ref in ((kv, mine_ref), (1 - kv, give_ref)):
        at = pl.ds(pl.multiple_of(core * rows, rows), rows)
        total = running_ref[at, :].astype(jnp.float32) + term_ref[at, :].astype(jnp.float32)
        ref[...] = total.astype(ref.dtype)


def share(place, running, term):
    rows, columns = running.shape
    whole = pl.BlockSpec(memory_space=pltpu.VMEM)
    return pl.pallas_call(
        share_kernel,
        in_specs=[pl.BlockSpec(memory_space=pltpu.SMEM)] + [whole] * 2,
        out_specs=[whole] * 2,
        out_shape=[jax.ShapeDtypeStruct((rows // 2, columns), running.dtype)] * 2,
        compiler_params=pltpu.CompilerParams(vmem_limit_bytes=4 * MIB),
        name="share",
    )(place, running, term)


def collect_kernel(place_ref, *refs):
    out_ref = refs[-1]
    width = refs[0].shape[1]
    req, kv = place_ref[0], place_ref[1]
    of = (2 * req + kv, 2 * req + 1 - kv, 2 - 2 * req + kv, 3 - 2 * req - kv)
    for quarter, ref in zip(of, refs[:-1]):
        out_ref[0, :, pl.ds(pl.multiple_of(quarter * width, width), width)] = ref[...]


def collect(place, *quarters):
    rows, columns = quarters[0].shape
    whole = pl.BlockSpec(memory_space=pltpu.VMEM)
    return pl.pallas_call(
        collect_kernel,
        in_specs=[pl.BlockSpec(memory_space=pltpu.SMEM)] + [whole] * 4,
        out_specs=whole,
        out_shape=jax.ShapeDtypeStruct((1, rows, 4 * columns), quarters[0].dtype),
        compiler_params=pltpu.CompilerParams(vmem_limit_bytes=4 * MIB),
        name="collect",
    )(place, *quarters)


def project_kernel(flips, place_ref, *refs):
    outputs = len(flips)
    pieces = refs[: -3 - outputs]
    q_ref, k_ref, v_ref = refs[-3 - outputs : -outputs]
    outs = refs[-outputs:]
    x = jnp.concatenate([piece[...] for piece in pieces], axis=0)
    head_dim = k_ref.shape[1] // 2
    width = 256
    base = q_ref.shape[1] // 2
    for number, out in enumerate(outs):
        kv = place_ref[1]
        half = 1 - kv if flips[number] else kv
        for t in range(base // width):
            at = pl.multiple_of(half * base + t * width, width)
            product = jnp.dot(x, q_ref[:, pl.ds(at, width)], preferred_element_type=jnp.float32)
            out[:, t * width : (t + 1) * width] = product.astype(out.dtype)
        at = pl.ds(pl.multiple_of(half * head_dim, head_dim), head_dim)
        both = jnp.concatenate((k_ref[:, at], v_ref[:, at]), axis=1)
        product = jnp.dot(x, both, preferred_element_type=jnp.float32)
        out[:, base:] = product.astype(out.dtype)


def project(place, pieces, weights, flips, kinds):
    rows = sum(piece.shape[0] for piece in pieces)
    total = sum(w.shape[1] for w in weights) // 2
    whole = pl.BlockSpec(memory_space=pltpu.VMEM)
    return pl.pallas_call(
        functools.partial(project_kernel, flips),
        in_specs=[pl.BlockSpec(memory_space=pltpu.SMEM)] + [whole] * (len(pieces) + 3),
        out_specs=[whole] * len(kinds),
        out_shape=[jax.ShapeDtypeStruct((rows, total), kind) for kind in kinds],
        compiler_params=pltpu.CompilerParams(vmem_limit_bytes=6 * MIB),
        name="project",
    )(place, *pieces, *weights)


def out_kernel(place_ref, own_ref, other_ref, w_ref, *outs):
    depth = own_ref.shape[1]
    part = own_ref.shape[0] // len(outs)
    mine = place_ref[1]
    at = pl.multiple_of(mine * depth, depth)
    off = pl.multiple_of((1 - mine) * depth, depth)
    own, other = own_ref[...], other_ref[...]
    width = 256
    for t in range(w_ref.shape[1] // width):
        columns = slice(t * width, (t + 1) * width)
        product = jnp.dot(
            own, w_ref[pl.ds(at, depth), columns], preferred_element_type=jnp.float32
        )
        product += jnp.dot(
            other, w_ref[pl.ds(off, depth), columns], preferred_element_type=jnp.float32
        )
        product = product.astype(outs[0].dtype)
        for j, out in enumerate(outs):
            out[:, columns] = product[j * part : (j + 1) * part]


def out_project(place, own, other, w_out, pieces):
    rows = own.shape[0]
    columns = w_out.shape[1]
    whole = pl.BlockSpec(memory_space=pltpu.VMEM)
    return pl.pallas_call(
        out_kernel,
        in_specs=[pl.BlockSpec(memory_space=pltpu.SMEM)] + [whole] * 3,
        out_specs=[whole] * pieces,
        out_shape=[jax.ShapeDtypeStruct((rows // pieces, columns), jnp.bfloat16)] * pieces,
        compiler_params=pltpu.CompilerParams(vmem_limit_bytes=6 * MIB),
        name="out_project",
    )(place, own, other, w_out)


def attend_kernel(wanted, order, place_ref, ids_ref, seg_ref, keep_ref, *refs):
    come_refs, (chip_ref, away_ref, out_ref) = refs[:-3], refs[-3:]
    req, kv, tp = place_ref[0], place_ref[1], place_ref[2]
    groups = 2
    steps = ids_ref.shape[1]
    total_cols = keep_ref.shape[1]
    rows = keep_ref.shape[0] // groups
    part = out_ref.shape[0] // (groups * len(wanted))
    pieces = rows // part
    some = part * len(wanted)
    head_dim = chip_ref.shape[-1]
    blocks, length = chip_ref.shape[2:4]
    heads = total_cols // head_dim - 2
    q_cols = heads * head_dim
    scale = head_dim**-0.5
    stack = min(heads, max(1, 256 // some))
    chain = CHAIN_BLOCKS * length

    def looked_up(index, options):
        result = jnp.int32(options[0])
        for number, option in enumerate(options[1:], 1):
            result = jnp.where(index == number, jnp.int32(option), result)
        return result

    spot = looked_up(tp, [order.index(i) for i in range(pieces)])
    source = [looked_up(lax.rem(spot - j + pieces, pieces), order) for j in range(pieces)]

    def branch(block, which):
        device = block // blocks
        near = device // 2 == req
        core = jnp.where(lax.rem(device, 2) == kv, 0, 1)
        at = lax.rem(block, blocks)
        here = chip_ref[core, which, pl.ds(at, CHAIN_BLOCKS)]
        there = away_ref[core, which, pl.ds(at, CHAIN_BLOCKS)]
        return jnp.where(near, here, there).reshape(chain, head_dim)

    def position(index, sources):
        piece = index // part
        start = jnp.full(index.shape, source[sources[0]], jnp.int32)
        for j in range(1, len(sources)):
            start = jnp.where(piece == j, source[sources[j]], start)
        return start * part + index % part

    row_pos = position(lax.broadcasted_iota(jnp.int32, (some, rows), 0), wanted)
    across = lax.broadcasted_iota(jnp.int32, (some, rows), 1)
    col_pos = position(across, range(pieces))
    come = jnp.concatenate([ref[...] for ref in come_refs], axis=0)
    whole = (keep_ref[...] + come.astype(jnp.float32)).astype(jnp.bfloat16)

    def own_rows(g, j, columns):
        at = (j * groups + g) * part
        return whole[at : at + part, columns]

    for g in range(groups):
        group = 2 * req + g
        segments = seg_ref[pl.ds(group, 1), :]
        root = jnp.int32(0)
        keys, values = [branch(root, 0)], [branch(root, 1)]
        bias = [jnp.zeros((some, chain), jnp.float32)]
        same = None
        low = jnp.int32(0)
        for s in range(steps):
            first = ids_ref[group, s, ROOT_BLOCKS]
            count = jnp.int32(0)
            for slot in range(CHAIN_BLOCKS):
                count += jnp.where(ids_ref[group, s, ROOT_BLOCKS + slot] >= 0, length, 0)
            high = jnp.sum((segments <= s).astype(jnp.int32))
            keys.append(branch(first, 0))
            values.append(branch(first, 1))
            row_in = (row_pos >= low) & (row_pos < high)
            col_in = (col_pos >= low) & (col_pos < high)
            both = row_in & col_in
            same = both if same is None else same | both
            for piece in range(chain // rows):
                allowed = row_in & (across + piece * rows < count)
                bias.append(jnp.where(allowed, 0.0, MASKED))
            low = high
        for j in range(pieces):
            keys.append(own_rows(g, j, slice(q_cols, q_cols + head_dim)))
            values.append(own_rows(g, j, slice(q_cols + head_dim, None)))
        bias.append(jnp.where(same & (col_pos <= row_pos), 0.0, MASKED))
        keys = jnp.concatenate(keys, axis=0)
        values = jnp.concatenate(values, axis=0)
        bias = jnp.concatenate(bias, axis=1)
        bias = jnp.concatenate([bias] * stack, axis=0)
        for low_head in range(0, heads, stack):
            query = jnp.concatenate(
                [
                    own_rows(g, j, slice(h * head_dim, (h + 1) * head_dim))
                    for h in range(low_head, low_head + stack)
                    for j in wanted
                ],
                axis=0,
            )
            scores = lax.dot_general(
                query, keys, (((1,), (1,)), ((), ())), preferred_element_type=jnp.float32
            )
            scores = scores * scale + bias
            top = jnp.max(scores, axis=1, keepdims=True)
            weights = jnp.exp(scores - top)
            total = jnp.sum(weights, axis=1, keepdims=True)
            summed = jnp.dot(
                weights.astype(jnp.bfloat16), values, preferred_element_type=jnp.float32
            )
            result = (summed / total).astype(out_ref.dtype)
            for n in range(stack):
                columns = slice((low_head + n) * head_dim, (low_head + n + 1) * head_dim)
                for number in range(len(wanted)):
                    of, to = n * some + number * part, (number * groups + g) * part
                    out_ref[to : to + part, columns] = result[of : of + part]


def attend(wanted, order, place, ids, segments, keep, come, chip, away, part):
    rows = 2 * len(wanted) * part
    whole = pl.BlockSpec(memory_space=pltpu.VMEM)
    scalars = pl.BlockSpec(memory_space=pltpu.SMEM)
    return pl.pallas_call(
        functools.partial(attend_kernel, wanted, order),
        in_specs=[scalars] * 2 + [whole] * (len(come) + 4),
        out_specs=whole,
        out_shape=jax.ShapeDtypeStruct((rows, keep.shape[1] - 2 * HD), jnp.bfloat16),
        compiler_params=pltpu.CompilerParams(vmem_limit_bytes=10 * MIB),
        name="attend",
    )(place, ids, segments, keep, *come, chip, away)


ROOT_BLOCKS = 4
CHAIN_BLOCKS = 4


def on_device(
    tokens, norm_gain, w_query, w_key, w_value, w_out, cache_keys, cache_values, seg_ids, block_ids
):
    req, kv, tp = lax.axis_index("req"), lax.axis_index("kv"), lax.axis_index("tp")
    part = tokens.shape[1]
    count = lax.axis_size("tp")
    order = tp_ring(count)
    forward = [(order[i], order[(i + 1) % count]) for i in range(count)]
    place = jnp.stack((req, kv, tp)).astype(jnp.int32)

    def swap_req(x):
        return lax.ppermute(x, "req", SWAP)

    def swap_kv(x):
        return lax.ppermute(x, "kv", SWAP)

    def swap_both(x):
        return lax.ppermute(x, ("req", "kv"), [(i, 3 - i) for i in range(4)])

    def onward(x):
        return lax.ppermute(x, "tp", forward)

    kept, give, far_same, far_cross = norm(place, tokens, norm_gain)
    near = merge(place, kept, swap_kv(give))
    far = merge(place, swap_req(far_same), swap_both(far_cross))

    near_pieces, far_pieces = [near, onward(near)], [far]
    weights = load(46, *after((w_query, w_key, w_value), near))
    far_pieces.append(onward(after(far, weights)))
    mine, give = cached_heads(place, *after((cache_keys, cache_values), weights))
    chip = jnp.stack((mine, swap_kv(give)))
    away = swap_req(chip)
    for pieces in (near_pieces, far_pieces):
        for _ in range(count - 2):
            pieces.append(onward(pieces[-1]))

    kinds = (jnp.bfloat16, jnp.float32)

    def summed(sent, kept, kind):
        return (kept + swap_kv(sent).astype(jnp.float32)).astype(kind)

    near_terms = project(place, after(near_pieces, away), weights, (True, False), kinds)
    keep = summed(*near_terms, jnp.float32)
    far_pieces = after(far_pieces, near_terms)
    sent = project(place, far_pieces, weights, (True,), kinds[:1])
    kept = project(place, far_pieces, weights, (False,), kinds[1:])
    far_terms = summed(*sent, *kept, jnp.bfloat16)
    come = (swap_req(far_terms),)
    w_out = load(38, *after((w_out,), far_terms))[0]

    middle = count // 2
    halves = (tuple(range(1, middle + 1)), tuple(j % count for j in range(middle + 1, count + 1)))
    near_sum, far_sum = {}, {}

    def attended(wanted, *gates):
        inputs = after(keep, *gates)
        return attend(
            wanted, order, place, block_ids, seg_ids, inputs, come, chip, away, part
        )

    def projected(sums, wanted, own, other):
        sums |= zip(wanted, out_project(place, own, other, w_out, middle))

    def plus(running, term):
        return (running.astype(jnp.float32) + term.astype(jnp.float32)).astype(jnp.bfloat16)

    rows = attended(halves[0], w_out)
    rows_far = swap_req(rows)
    projected(near_sum, halves[0], rows, swap_kv(rows))
    near_run = onward(near_sum[1])
    last = attended(halves[1], near_sum[1])
    last_far = swap_req(last)
    rows_far = after(rows_far, last)
    rows_far = after((rows_far, swap_kv(rows_far)), near_run)
    projected(far_sum, halves[0], *rows_far)
    far_run = onward(far_sum[1])
    projected(near_sum, halves[1], last, swap_kv(last))
    last_far = after(last_far, near_run)
    projected(far_sum, halves[1], last_far, swap_kv(last_far))
    for j in range(2, count):
        near_term = plus(near_run, near_sum[j])
        near_run = onward(after(near_term, far_run) if j == count - 1 else near_term)
        far_run = onward(plus(far_run, far_sum[j]))
    mine, give = share(place, far_run, far_sum[0])
    away = (swap_req(mine), swap_both(give))
    mine, give = share(place, near_run, near_sum[0])
    return collect(place, mine, swap_kv(give), *away)


def fits(shape):
    local_kv = KVH // shape["tp"]
    return shape["req"] == 2 and shape["kv"] == 2 and shape["tp"] > 1 and local_kv == 2


def solution(mesh):
    placed = (
        P(("grp", "req", "kv"), "tp", None),
        P(),
        P(("req", "kv"), "tp"),
        P(("req", "kv"), "tp"),
        P(("req", "kv"), "tp"),
        P("tp", ("req", "kv")),
        P(("grp", "req", "kv"), None, None),
        P(("grp", "req", "kv"), None, None),
        P("grp", None),
        P("grp", None, None),
    )
    return jax.shard_map(
        on_device if fits(mesh.shape) else general_path,
        mesh=mesh,
        in_specs=placed,
        out_specs=P(("grp", "req", "kv"), "tp", None),
        check_vma=False,
    )
```

```python
import functools

import jax
import jax.numpy as jnp
from jax import lax
from jax.experimental import pallas as pl
from jax.experimental.pallas import tpu as pltpu
from jax.sharding import PartitionSpec as P

HQ = 64
KVH = 8
HD = 128


EPS = 1e-06


def swapped(block, axis, distance):
    count = lax.axis_size(axis)
    route = []
    for low in range(count):
        high = low | 1 << distance
        if high != low and high < count:
            route += [(low, high), (high, low)]
    return lax.ppermute(block, axis, route)


def combined_all(shard, axis, join):
    gathered = jax.tree.map(
        lambda a, kind: lax.all_gather(a.astype(kind), axis),
        shard,
        jax.tree.map(lambda a: jnp.bfloat16 if a.dtype == jnp.float32 else a.dtype, shard),
    )

    def take(source):
        return jax.tree.map(
            lambda a, own: lax.dynamic_index_in_dim(a, source, 0, False).astype(own.dtype),
            gathered,
            shard,
        )

    return lax.fori_loop(
        1, lax.axis_size(axis), lambda source, state: join(state, take(source)), take(0)
    )


def partial_attend(heads, keys, values, allowed, scale):
    scores = jnp.einsum("rkgd,nkd->rkgn", heads, keys, preferred_element_type=jnp.float32) * scale
    wide_mask = allowed[:, None, None, :]
    scores = jnp.where(wide_mask, scores, -1e30)
    top = jnp.max(scores, axis=-1)
    weights = jnp.where(wide_mask, jnp.exp(scores - top[..., None]), 0.0)
    total = jnp.sum(weights, axis=-1)
    summed = jnp.einsum(
        "rkgn,nkd->rkgd", weights.astype(jnp.bfloat16), values, preferred_element_type=jnp.float32
    )
    return (top, total, summed)


def combine(first, second):
    top = jnp.maximum(first[0], second[0])
    left = jnp.exp(first[0] - top)
    right = jnp.exp(second[0] - top)
    return (
        top,
        first[1] * left + second[1] * right,
        first[2] * left[..., None] + second[2] * right[..., None],
    )


def general_path(
    tokens, norm_gain, w_query, w_key, w_value, w_out, cache_keys, cache_values, seg_ids, block_ids
):
    groups = seg_ids.shape[0]
    rows = seg_ids.shape[1]
    steps = block_ids.shape[1]
    group = lax.axis_index(("req", "kv"))
    tp_index = lax.axis_index("tp")
    head_dim = HD
    gsize = HQ // KVH
    local_heads = w_query.shape[1] // head_dim
    per_kv = min(gsize, local_heads)
    kv_count = local_heads // per_kv
    first_kv = tp_index * local_heads // gsize
    scale = head_dim ** (-0.5)
    blocks_here = cache_keys.shape[0]
    block_len = cache_keys.shape[1]
    blocks_all = blocks_here * groups
    wide = tokens[0].astype(jnp.float32)
    normed = (
        wide
        * lax.rsqrt(jnp.mean(wide * wide, axis=-1, keepdims=True) + EPS)
        * norm_gain.astype(jnp.float32)
    ).astype(jnp.bfloat16)
    whole = lax.all_gather(normed, "tp", axis=0, tiled=True)
    pieces = (
        lax.all_gather(w_query, ("req", "kv"), axis=0, tiled=True),
        lax.all_gather(w_key, ("req", "kv"), axis=0, tiled=True),
        lax.all_gather(w_value, ("req", "kv"), axis=0, tiled=True),
    )
    query_acc, key_acc, value_acc = tuple(
        (jnp.dot(whole, piece, preferred_element_type=jnp.float32) for piece in pieces)
    )
    queries = query_acc.astype(jnp.bfloat16)
    span = max(1, gsize // local_heads)
    stacked = jnp.stack((key_acc.astype(jnp.bfloat16), value_acc.astype(jnp.bfloat16)))
    for bit in range(span.bit_length() - 1):
        partner = swapped(stacked, "tp", bit)
        upper = tp_index // (1 << bit) % 2 == 1
        stacked = jnp.where(
            upper, jnp.concatenate((partner, stacked), 2), jnp.concatenate((stacked, partner), 2)
        )
    own_keys = stacked[0].reshape(rows, kv_count, head_dim)
    own_values = stacked[1].reshape(rows, kv_count, head_dim)
    heads = queries.reshape(rows, kv_count, per_kv, head_dim)
    member = jnp.any(
        block_ids[..., None] == jnp.arange(blocks_all, dtype=jnp.int32), axis=-2
    ).astype(jnp.float32)
    onehot = (seg_ids[..., None] == jnp.arange(steps, dtype=jnp.int32)).astype(jnp.float32)
    block_mask = jnp.einsum("grs,gsb->grb", onehot, member) > 0.5
    seg_here = lax.dynamic_index_in_dim(seg_ids, group, 0, keepdims=False)
    places = jnp.arange(rows, dtype=jnp.int32)
    own_mask = (seg_here[:, None] == seg_here[None, :]) & (places[:, None] >= places[None, :])
    own_part = partial_attend(heads, own_keys, own_values, own_mask, scale)
    gathered = lax.all_gather(queries[None], ("req", "kv"), axis=0, tiled=True)
    all_heads = gathered.reshape(groups * rows, kv_count, per_kv, head_dim)
    local_keys = lax.dynamic_slice_in_dim(
        cache_keys, first_kv * head_dim, kv_count * head_dim, 2
    ).reshape(blocks_here * block_len, kv_count, head_dim)
    local_values = lax.dynamic_slice_in_dim(
        cache_values, first_kv * head_dim, kv_count * head_dim, 2
    ).reshape(blocks_here * block_len, kv_count, head_dim)
    local_blocks = lax.dynamic_slice_in_dim(
        block_mask, group * blocks_here, blocks_here, 2
    ).reshape(groups * rows, blocks_here)
    local_mask = jnp.repeat(local_blocks, block_len, axis=1)
    cache_part = partial_attend(all_heads, local_keys, local_values, local_mask, scale)
    merged = combined_all(cache_part, ("req", "kv"), combine)
    mine = tuple((lax.dynamic_slice_in_dim(item, group * rows, rows, 0) for item in merged))
    top, total, summed = combine(mine, own_part)
    attended = (
        (summed / total[..., None]).astype(jnp.bfloat16).reshape(rows, local_heads * head_dim)
    )
    out_full = lax.all_gather(w_out, ("req", "kv"), axis=1, tiled=True)
    branch = lax.psum_scatter(
        jnp.dot(attended, out_full, preferred_element_type=jnp.float32).astype(jnp.bfloat16),
        "tp",
        scatter_dimension=0,
        tiled=True,
    )
    return branch[None]


SWAP = [(0, 1), (1, 0)]
MASKED = -1e30
MIB = 2**20


def tp_ring(count):
    return list(range(0, count, 2)) + list(range(1, count, 2))[::-1]


def after(value, *gates):
    if not gates:
        return value
    return lax.optimization_barrier((value, gates))[0]


def norm_kernel(place_ref, x_ref, gain_ref, keep_ref, give_ref, far_ref, cross_ref):
    wide = x_ref[0].astype(jnp.float32)
    factor = lax.rsqrt(jnp.mean(wide * wide, axis=1, keepdims=True) + EPS)
    width = keep_ref.shape[1]
    req, kv = place_ref[0], place_ref[1]
    to = (2 * req + kv, 2 * req + 1 - kv, 2 - 2 * req + kv, 3 - 2 * req - kv)
    for quarter, ref in zip(to, (keep_ref, give_ref, far_ref, cross_ref)):
        at = pl.multiple_of(quarter * width, width)
        part = x_ref[0, :, pl.ds(at, width)].astype(jnp.float32)
        gain = gain_ref[:, pl.ds(at, width)].astype(jnp.float32)
        ref[...] = (part * factor * gain).astype(ref.dtype)


def norm(place, tokens, gain):
    rows, depth = tokens.shape[1:]
    whole = pl.BlockSpec(memory_space=pltpu.VMEM)
    quarter = jax.ShapeDtypeStruct((rows, depth // 4), jnp.bfloat16)
    return pl.pallas_call(
        norm_kernel,
        in_specs=[pl.BlockSpec(memory_space=pltpu.SMEM), whole, whole],
        out_specs=[whole] * 4,
        out_shape=[quarter] * 4,
        compiler_params=pltpu.CompilerParams(vmem_limit_bytes=4 * MIB),
        name="norm",
    )(place, tokens, gain.reshape(1, depth))


def load_kernel(count, *refs):
    copies = [
        pltpu.make_async_copy(source, to, refs[-1].at[number])
        for number, (source, to) in enumerate(zip(refs[:count], refs[count:]))
    ]
    for copy in copies:
        copy.start()
    for copy in copies:
        copy.wait()


def load(limit, *arrays):
    count = len(arrays)
    return pl.pallas_call(
        functools.partial(load_kernel, count),
        in_specs=[pl.BlockSpec(memory_space=pl.ANY)] * count,
        out_specs=[pl.BlockSpec(memory_space=pltpu.VMEM)] * count,
        out_shape=[pltpu.VMEM(a.shape, a.dtype) for a in arrays],
        scratch_shapes=[pltpu.SemaphoreType.DMA((count,))],
        compiler_params=pltpu.CompilerParams(vmem_limit_bytes=limit * MIB),
        name="load",
    )(*arrays)


def heads_kernel(place_ref, k_ref, v_ref, mine_ref, give_ref, sems):
    head_dim = mine_ref.shape[-1]
    kv, tp = place_ref[1], place_ref[2]
    copies = []
    for number, (out, core) in enumerate(((mine_ref, kv), (give_ref, 1 - kv))):
        at = pl.multiple_of((2 * tp + core) * head_dim, head_dim)
        for which, ref in enumerate((k_ref, v_ref)):
            copies.append(
                pltpu.make_async_copy(
                    ref.at[:, :, pl.ds(at, head_dim)], out.at[which], sems.at[2 * number + which]
                )
            )
    for copy in copies:
        copy.start()
    for copy in copies:
        copy.wait()


def cached_heads(place, keys, values):
    blocks, length = keys.shape[:2]
    out = jax.ShapeDtypeStruct((2, blocks, length, HD), keys.dtype)
    return pl.pallas_call(
        heads_kernel,
        in_specs=[pl.BlockSpec(memory_space=pltpu.SMEM)]
        + [pl.BlockSpec(memory_space=pl.ANY)] * 2,
        out_specs=[pl.BlockSpec(memory_space=pltpu.VMEM)] * 2,
        out_shape=[out] * 2,
        scratch_shapes=[pltpu.SemaphoreType.DMA((4,))],
        compiler_params=pltpu.CompilerParams(vmem_limit_bytes=4 * MIB),
        name="cached_heads",
    )(place, keys, values)


def merge_kernel(place_ref, mine_ref, theirs_ref, out_ref):
    rows = mine_ref.shape[0]
    kv = place_ref[1]
    out_ref[pl.ds(pl.multiple_of(kv * rows, rows), rows), :] = mine_ref[...]
    out_ref[pl.ds(pl.multiple_of((1 - kv) * rows, rows), rows), :] = theirs_ref[...]


def merge(place, mine, theirs):
    rows, columns = mine.shape
    whole = pl.BlockSpec(memory_space=pltpu.VMEM)
    return pl.pallas_call(
        merge_kernel,
        in_specs=[pl.BlockSpec(memory_space=pltpu.SMEM)] + [whole] * 2,
        out_specs=whole,
        out_shape=jax.ShapeDtypeStruct((2 * rows, columns), mine.dtype),
        compiler_params=pltpu.CompilerParams(vmem_limit_bytes=4 * MIB),
        name="merge",
    )(place, mine, theirs)


def share_kernel(place_ref, *refs):
    terms, (mine_ref, give_ref) = refs[:-2], refs[-2:]
    rows = mine_ref.shape[0]
    kv = place_ref[1]
    for core, ref in ((kv, mine_ref), (1 - kv, give_ref)):
        at = pl.ds(pl.multiple_of(core * rows, rows), rows)
        total = sum(term[at, :].astype(jnp.float32) for term in terms)
        ref[...] = total.astype(ref.dtype)


def share(place, *terms):
    rows, columns = terms[0].shape
    whole = pl.BlockSpec(memory_space=pltpu.VMEM)
    return pl.pallas_call(
        share_kernel,
        in_specs=[pl.BlockSpec(memory_space=pltpu.SMEM)] + [whole] * len(terms),
        out_specs=[whole] * 2,
        out_shape=[jax.ShapeDtypeStruct((rows // 2, columns), terms[0].dtype)] * 2,
        compiler_params=pltpu.CompilerParams(vmem_limit_bytes=4 * MIB),
        name="share",
    )(place, *terms)


def collect_kernel(place_ref, *refs):
    terms, out_ref = refs[:-1], refs[-1]
    width = terms[0].shape[1]
    req, kv = place_ref[0], place_ref[1]
    of = (2 * req + kv, 2 * req + 1 - kv, 2 - 2 * req + kv, 3 - 2 * req - kv)
    pairs = (terms[:1], terms[1:2], terms[2:4], terms[4:])
    for quarter, pair in zip(of, pairs):
        total = sum(term[...].astype(jnp.float32) for term in pair)
        at = pl.ds(pl.multiple_of(quarter * width, width), width)
        out_ref[0, :, at] = total.astype(out_ref.dtype)


def collect(place, mine, theirs, same, cross):
    rows, columns = mine.shape
    whole = pl.BlockSpec(memory_space=pltpu.VMEM)
    return pl.pallas_call(
        collect_kernel,
        in_specs=[pl.BlockSpec(memory_space=pltpu.SMEM)] + [whole] * 6,
        out_specs=whole,
        out_shape=jax.ShapeDtypeStruct((1, rows, 4 * columns), mine.dtype),
        compiler_params=pltpu.CompilerParams(vmem_limit_bytes=4 * MIB),
        name="collect",
    )(place, mine, theirs, *same, *cross)


def project_kernel(flips, place_ref, *refs):
    outputs = len(flips)
    pieces = refs[: -3 - outputs]
    q_ref, k_ref, v_ref = refs[-3 - outputs : -outputs]
    outs = refs[-outputs:]
    x = jnp.concatenate([piece[...] for piece in pieces], axis=0)
    head_dim = k_ref.shape[1] // 2
    width = 256
    base = q_ref.shape[1] // 2
    for number, out in enumerate(outs):
        kv = place_ref[1]
        half = 1 - kv if flips[number] else kv
        for t in range(base // width):
            at = pl.multiple_of(half * base + t * width, width)
            product = jnp.dot(x, q_ref[:, pl.ds(at, width)], preferred_element_type=jnp.float32)
            out[:, t * width : (t + 1) * width] = product.astype(out.dtype)
        at = pl.ds(pl.multiple_of(half * head_dim, head_dim), head_dim)
        both = jnp.concatenate((k_ref[:, at], v_ref[:, at]), axis=1)
        product = jnp.dot(x, both, preferred_element_type=jnp.float32)
        out[:, base:] = product.astype(out.dtype)


def project(place, pieces, weights, flips, kinds):
    rows = sum(piece.shape[0] for piece in pieces)
    total = sum(w.shape[1] for w in weights) // 2
    whole = pl.BlockSpec(memory_space=pltpu.VMEM)
    return pl.pallas_call(
        functools.partial(project_kernel, flips),
        in_specs=[pl.BlockSpec(memory_space=pltpu.SMEM)] + [whole] * (len(pieces) + 3),
        out_specs=[whole] * len(kinds),
        out_shape=[jax.ShapeDtypeStruct((rows, total), kind) for kind in kinds],
        compiler_params=pltpu.CompilerParams(vmem_limit_bytes=6 * MIB),
        name="project",
    )(place, *pieces, *weights)


def out_kernel(place_ref, own_ref, other_ref, w_ref, *outs):
    depth = own_ref.shape[1]
    part = own_ref.shape[0] // len(outs)
    mine = place_ref[1]
    at = pl.multiple_of(mine * depth, depth)
    off = pl.multiple_of((1 - mine) * depth, depth)
    own, other = own_ref[...], other_ref[...]
    width = 256
    for t in range(w_ref.shape[1] // width):
        columns = slice(t * width, (t + 1) * width)
        product = jnp.dot(
            own, w_ref[pl.ds(at, depth), columns], preferred_element_type=jnp.float32
        )
        product += jnp.dot(
            other, w_ref[pl.ds(off, depth), columns], preferred_element_type=jnp.float32
        )
        product = product.astype(outs[0].dtype)
        for j, out in enumerate(outs):
            out[:, columns] = product[j * part : (j + 1) * part]


def out_project(place, own, other, w_out, pieces):
    rows = own.shape[0]
    columns = w_out.shape[1]
    whole = pl.BlockSpec(memory_space=pltpu.VMEM)
    return pl.pallas_call(
        out_kernel,
        in_specs=[pl.BlockSpec(memory_space=pltpu.SMEM)] + [whole] * 3,
        out_specs=[whole] * pieces,
        out_shape=[jax.ShapeDtypeStruct((rows // pieces, columns), jnp.bfloat16)] * pieces,
        compiler_params=pltpu.CompilerParams(vmem_limit_bytes=6 * MIB),
        name="out_project",
    )(place, own, other, w_out)


def attend_kernel(wanted, order, place_ref, ids_ref, seg_ref, keep_ref, *refs):
    come_refs, (chip_ref, away_ref, out_ref) = refs[:-3], refs[-3:]
    req, kv, tp = place_ref[0], place_ref[1], place_ref[2]
    groups = 2
    steps = ids_ref.shape[1]
    total_cols = keep_ref.shape[1]
    rows = keep_ref.shape[0] // groups
    part = out_ref.shape[0] // (groups * len(wanted))
    pieces = rows // part
    some = part * len(wanted)
    head_dim = chip_ref.shape[-1]
    blocks, length = chip_ref.shape[2:4]
    heads = total_cols // head_dim - 2
    q_cols = heads * head_dim
    scale = head_dim**-0.5
    stack = min(heads, max(1, 256 // some))
    chain = CHAIN_BLOCKS * length

    def looked_up(index, options):
        result = jnp.int32(options[0])
        for number, option in enumerate(options[1:], 1):
            result = jnp.where(index == number, jnp.int32(option), result)
        return result

    spot = looked_up(tp, [order.index(i) for i in range(pieces)])
    source = [looked_up(lax.rem(spot - j + pieces, pieces), order) for j in range(pieces)]

    def branch(block, which):
        device = block // blocks
        near = device // 2 == req
        core = jnp.where(lax.rem(device, 2) == kv, 0, 1)
        at = lax.rem(block, blocks)
        here = chip_ref[core, which, pl.ds(at, CHAIN_BLOCKS)]
        there = away_ref[core, which, pl.ds(at, CHAIN_BLOCKS)]
        return jnp.where(near, here, there).reshape(chain, head_dim)

    def position(index, sources):
        piece = index // part
        start = jnp.full(index.shape, source[sources[0]], jnp.int32)
        for j in range(1, len(sources)):
            start = jnp.where(piece == j, source[sources[j]], start)
        return start * part + index % part

    row_pos = position(lax.broadcasted_iota(jnp.int32, (some, rows), 0), wanted)
    across = lax.broadcasted_iota(jnp.int32, (some, rows), 1)
    col_pos = position(across, range(pieces))
    come = jnp.concatenate([ref[...] for ref in come_refs], axis=0)
    whole = (keep_ref[...] + come.astype(jnp.float32)).astype(jnp.bfloat16)

    def own_rows(g, j, columns):
        at = (j * groups + g) * part
        return whole[at : at + part, columns]

    for g in range(groups):
        group = 2 * req + g
        segments = seg_ref[pl.ds(group, 1), :]
        root = jnp.int32(0)
        keys, values = [branch(root, 0)], [branch(root, 1)]
        bias = [jnp.zeros((some, chain), jnp.float32)]
        same = None
        low = jnp.int32(0)
        for s in range(steps):
            first = ids_ref[group, s, ROOT_BLOCKS]
            count = jnp.int32(0)
            for slot in range(CHAIN_BLOCKS):
                count += jnp.where(ids_ref[group, s, ROOT_BLOCKS + slot] >= 0, length, 0)
            high = jnp.sum((segments <= s).astype(jnp.int32))
            keys.append(branch(first, 0))
            values.append(branch(first, 1))
            row_in = (row_pos >= low) & (row_pos < high)
            col_in = (col_pos >= low) & (col_pos < high)
            both = row_in & col_in
            same = both if same is None else same | both
            for piece in range(chain // rows):
                allowed = row_in & (across + piece * rows < count)
                bias.append(jnp.where(allowed, 0.0, MASKED))
            low = high
        for j in range(pieces):
            keys.append(own_rows(g, j, slice(q_cols, q_cols + head_dim)))
            values.append(own_rows(g, j, slice(q_cols + head_dim, None)))
        bias.append(jnp.where(same & (col_pos <= row_pos), 0.0, MASKED))
        keys = jnp.concatenate(keys, axis=0)
        values = jnp.concatenate(values, axis=0)
        bias = jnp.concatenate(bias, axis=1)
        bias = jnp.concatenate([bias] * stack, axis=0)
        for low_head in range(0, heads, stack):
            query = jnp.concatenate(
                [
                    own_rows(g, j, slice(h * head_dim, (h + 1) * head_dim))
                    for h in range(low_head, low_head + stack)
                    for j in wanted
                ],
                axis=0,
            )
            scores = lax.dot_general(
                query, keys, (((1,), (1,)), ((), ())), preferred_element_type=jnp.float32
            )
            scores = scores * scale + bias
            top = jnp.max(scores, axis=1, keepdims=True)
            weights = jnp.exp(scores - top)
            total = jnp.sum(weights, axis=1, keepdims=True)
            summed = jnp.dot(
                weights.astype(jnp.bfloat16), values, preferred_element_type=jnp.float32
            )
            result = (summed / total).astype(out_ref.dtype)
            for n in range(stack):
                columns = slice((low_head + n) * head_dim, (low_head + n + 1) * head_dim)
                for number in range(len(wanted)):
                    of, to = n * some + number * part, (number * groups + g) * part
                    out_ref[to : to + part, columns] = result[of : of + part]


def attend(wanted, order, place, ids, segments, keep, come, chip, away, part):
    rows = 2 * len(wanted) * part
    whole = pl.BlockSpec(memory_space=pltpu.VMEM)
    scalars = pl.BlockSpec(memory_space=pltpu.SMEM)
    return pl.pallas_call(
        functools.partial(attend_kernel, wanted, order),
        in_specs=[scalars] * 2 + [whole] * (len(come) + 4),
        out_specs=whole,
        out_shape=jax.ShapeDtypeStruct((rows, keep.shape[1] - 2 * HD), jnp.bfloat16),
        compiler_params=pltpu.CompilerParams(vmem_limit_bytes=10 * MIB),
        name="attend",
    )(place, ids, segments, keep, *come, chip, away)


ROOT_BLOCKS = 4
CHAIN_BLOCKS = 4


def on_device(
    tokens, norm_gain, w_query, w_key, w_value, w_out, cache_keys, cache_values, seg_ids, block_ids
):
    req, kv, tp = lax.axis_index("req"), lax.axis_index("kv"), lax.axis_index("tp")
    part = tokens.shape[1]
    count = lax.axis_size("tp")
    order = tp_ring(count)
    forward = [(order[i], order[(i + 1) % count]) for i in range(count)]
    place = jnp.stack((req, kv, tp)).astype(jnp.int32)

    def swap_req(x):
        return lax.ppermute(x, "req", SWAP)

    def swap_kv(x):
        return lax.ppermute(x, "kv", SWAP)

    def swap_both(x):
        return lax.ppermute(x, ("req", "kv"), [(i, 3 - i) for i in range(4)])

    def onward(x):
        return lax.ppermute(x, "tp", forward)

    def slanted(same, cross):
        axes = ("tp", "req", "kv")
        return [
            lax.ppermute(
                x,
                axes,
                [
                    (4 * low + 2 * r + c, 4 * high + 2 * (1 - r) + (c ^ flip))
                    for low, high in forward
                    for r in range(2)
                    for c in range(2)
                ],
            )
            for flip, x in enumerate((same, cross))
        ]

    kept, give, far_same, far_cross = norm(place, tokens, norm_gain)
    near = merge(place, kept, swap_kv(give))
    far = merge(place, swap_req(far_same), swap_both(far_cross))

    near_pieces, far_pieces = [near, onward(near)], [far]
    weights = load(46, *after((w_query, w_key, w_value), near))
    far_pieces.append(onward(after(far, weights)))
    mine, give = cached_heads(place, *after((cache_keys, cache_values), weights))
    chip = jnp.stack((mine, swap_kv(give)))
    away = swap_req(chip)
    for pieces in (near_pieces, far_pieces):
        for _ in range(count - 2):
            pieces.append(onward(pieces[-1]))

    kinds = (jnp.bfloat16, jnp.float32)

    def summed(sent, kept, kind):
        return (kept + swap_kv(sent).astype(jnp.float32)).astype(kind)

    near_terms = project(place, after(near_pieces, away), weights, (True, False), kinds)
    keep = summed(*near_terms, jnp.float32)
    far_pieces = after(far_pieces, near_terms)
    sent = project(place, far_pieces, weights, (True,), kinds[:1])
    kept = project(place, far_pieces, weights, (False,), kinds[1:])
    far_terms = summed(*sent, *kept, jnp.bfloat16)
    come = (swap_req(far_terms),)
    w_out = load(38, *after((w_out,), far_terms))[0]

    middle = count // 2
    halves = (tuple(range(1, middle + 1)), tuple(j % count for j in range(middle + 1, count + 1)))
    near_sum, far_sum = {}, {}

    def attended(wanted, *gates):
        inputs = after(keep, *gates)
        return attend(
            wanted, order, place, block_ids, seg_ids, inputs, come, chip, away, part
        )

    def projected(sums, wanted, own, other):
        sums |= zip(wanted, out_project(place, own, other, w_out, middle))

    def plus(running, term):
        return (running.astype(jnp.float32) + term.astype(jnp.float32)).astype(jnp.bfloat16)

    rows = attended(halves[0], w_out)
    rows_far = swap_req(rows)
    projected(near_sum, halves[0], rows, swap_kv(rows))
    near_run = onward(near_sum[1])
    last = attended(halves[1], near_sum[1])
    last_far = swap_req(last)
    rows_far = after(rows_far, last)
    rows_far = after((rows_far, swap_kv(rows_far)), near_run)
    projected(far_sum, halves[0], *rows_far)
    far_run = onward(far_sum[1])
    projected(near_sum, halves[1], last, swap_kv(last))
    last_far = after(last_far, near_run)
    projected(far_sum, halves[1], last_far, swap_kv(last_far))

    beside = share(place, after(far_sum[0], far_run))
    beside = (swap_req(beside[0]), swap_both(beside[1]))
    for j in range(2, count):
        near_run = onward(plus(near_run, near_sum[j]))
        if j < count - 1:
            far_run = onward(plus(far_run, far_sum[j]))
    ends = slanted(*share(place, far_run, far_sum[count - 1]))
    mine, give = share(place, near_run, near_sum[0])
    return collect(place, mine, swap_kv(give), *zip(ends, beside))


def fits(shape):
    local_kv = KVH // shape["tp"]
    return shape["req"] == 2 and shape["kv"] == 2 and shape["tp"] > 1 and local_kv == 2


def solution(mesh):
    placed = (
        P(("grp", "req", "kv"), "tp", None),
        P(),
        P(("req", "kv"), "tp"),
        P(("req", "kv"), "tp"),
        P(("req", "kv"), "tp"),
        P("tp", ("req", "kv")),
        P(("grp", "req", "kv"), None, None),
        P(("grp", "req", "kv"), None, None),
        P("grp", None),
        P("grp", None, None),
    )
    return jax.shard_map(
        on_device if fits(mesh.shape) else general_path,
        mesh=mesh,
        in_specs=placed,
        out_specs=P(("grp", "req", "kv"), "tp", None),
        check_vma=False,
    )
```

```python
import functools

import jax
import jax.numpy as jnp
from jax import lax
from jax.experimental import pallas as pl
from jax.experimental.pallas import tpu as pltpu
from jax.sharding import PartitionSpec as P

HQ = 64
KVH = 8
HD = 128


EPS = 1e-06


def swapped(block, axis, distance):
    count = lax.axis_size(axis)
    route = []
    for low in range(count):
        high = low | 1 << distance
        if high != low and high < count:
            route += [(low, high), (high, low)]
    return lax.ppermute(block, axis, route)


def combined_all(shard, axis, join):
    gathered = jax.tree.map(
        lambda a, kind: lax.all_gather(a.astype(kind), axis),
        shard,
        jax.tree.map(lambda a: jnp.bfloat16 if a.dtype == jnp.float32 else a.dtype, shard),
    )

    def take(source):
        return jax.tree.map(
            lambda a, own: lax.dynamic_index_in_dim(a, source, 0, False).astype(own.dtype),
            gathered,
            shard,
        )

    return lax.fori_loop(
        1, lax.axis_size(axis), lambda source, state: join(state, take(source)), take(0)
    )


def partial_attend(heads, keys, values, allowed, scale):
    scores = jnp.einsum("rkgd,nkd->rkgn", heads, keys, preferred_element_type=jnp.float32) * scale
    wide_mask = allowed[:, None, None, :]
    scores = jnp.where(wide_mask, scores, -1e30)
    top = jnp.max(scores, axis=-1)
    weights = jnp.where(wide_mask, jnp.exp(scores - top[..., None]), 0.0)
    total = jnp.sum(weights, axis=-1)
    summed = jnp.einsum(
        "rkgn,nkd->rkgd", weights.astype(jnp.bfloat16), values, preferred_element_type=jnp.float32
    )
    return (top, total, summed)


def combine(first, second):
    top = jnp.maximum(first[0], second[0])
    left = jnp.exp(first[0] - top)
    right = jnp.exp(second[0] - top)
    return (
        top,
        first[1] * left + second[1] * right,
        first[2] * left[..., None] + second[2] * right[..., None],
    )


def general_path(
    tokens, norm_gain, w_query, w_key, w_value, w_out, cache_keys, cache_values, seg_ids, block_ids
):
    groups = seg_ids.shape[0]
    rows = seg_ids.shape[1]
    steps = block_ids.shape[1]
    group = lax.axis_index(("req", "kv"))
    tp_index = lax.axis_index("tp")
    head_dim = HD
    gsize = HQ // KVH
    local_heads = w_query.shape[1] // head_dim
    per_kv = min(gsize, local_heads)
    kv_count = local_heads // per_kv
    first_kv = tp_index * local_heads // gsize
    scale = head_dim ** (-0.5)
    blocks_here = cache_keys.shape[0]
    block_len = cache_keys.shape[1]
    blocks_all = blocks_here * groups
    wide = tokens[0].astype(jnp.float32)
    normed = (
        wide
        * lax.rsqrt(jnp.mean(wide * wide, axis=-1, keepdims=True) + EPS)
        * norm_gain.astype(jnp.float32)
    ).astype(jnp.bfloat16)
    whole = lax.all_gather(normed, "tp", axis=0, tiled=True)
    pieces = (
        lax.all_gather(w_query, ("req", "kv"), axis=0, tiled=True),
        lax.all_gather(w_key, ("req", "kv"), axis=0, tiled=True),
        lax.all_gather(w_value, ("req", "kv"), axis=0, tiled=True),
    )
    query_acc, key_acc, value_acc = tuple(
        (jnp.dot(whole, piece, preferred_element_type=jnp.float32) for piece in pieces)
    )
    queries = query_acc.astype(jnp.bfloat16)
    span = max(1, gsize // local_heads)
    stacked = jnp.stack((key_acc.astype(jnp.bfloat16), value_acc.astype(jnp.bfloat16)))
    for bit in range(span.bit_length() - 1):
        partner = swapped(stacked, "tp", bit)
        upper = tp_index // (1 << bit) % 2 == 1
        stacked = jnp.where(
            upper, jnp.concatenate((partner, stacked), 2), jnp.concatenate((stacked, partner), 2)
        )
    own_keys = stacked[0].reshape(rows, kv_count, head_dim)
    own_values = stacked[1].reshape(rows, kv_count, head_dim)
    heads = queries.reshape(rows, kv_count, per_kv, head_dim)
    member = jnp.any(
        block_ids[..., None] == jnp.arange(blocks_all, dtype=jnp.int32), axis=-2
    ).astype(jnp.float32)
    onehot = (seg_ids[..., None] == jnp.arange(steps, dtype=jnp.int32)).astype(jnp.float32)
    block_mask = jnp.einsum("grs,gsb->grb", onehot, member) > 0.5
    seg_here = lax.dynamic_index_in_dim(seg_ids, group, 0, keepdims=False)
    places = jnp.arange(rows, dtype=jnp.int32)
    own_mask = (seg_here[:, None] == seg_here[None, :]) & (places[:, None] >= places[None, :])
    own_part = partial_attend(heads, own_keys, own_values, own_mask, scale)
    gathered = lax.all_gather(queries[None], ("req", "kv"), axis=0, tiled=True)
    all_heads = gathered.reshape(groups * rows, kv_count, per_kv, head_dim)
    local_keys = lax.dynamic_slice_in_dim(
        cache_keys, first_kv * head_dim, kv_count * head_dim, 2
    ).reshape(blocks_here * block_len, kv_count, head_dim)
    local_values = lax.dynamic_slice_in_dim(
        cache_values, first_kv * head_dim, kv_count * head_dim, 2
    ).reshape(blocks_here * block_len, kv_count, head_dim)
    local_blocks = lax.dynamic_slice_in_dim(
        block_mask, group * blocks_here, blocks_here, 2
    ).reshape(groups * rows, blocks_here)
    local_mask = jnp.repeat(local_blocks, block_len, axis=1)
    cache_part = partial_attend(all_heads, local_keys, local_values, local_mask, scale)
    merged = combined_all(cache_part, ("req", "kv"), combine)
    mine = tuple((lax.dynamic_slice_in_dim(item, group * rows, rows, 0) for item in merged))
    top, total, summed = combine(mine, own_part)
    attended = (
        (summed / total[..., None]).astype(jnp.bfloat16).reshape(rows, local_heads * head_dim)
    )
    out_full = lax.all_gather(w_out, ("req", "kv"), axis=1, tiled=True)
    branch = lax.psum_scatter(
        jnp.dot(attended, out_full, preferred_element_type=jnp.float32).astype(jnp.bfloat16),
        "tp",
        scatter_dimension=0,
        tiled=True,
    )
    return branch[None]


SWAP = [(0, 1), (1, 0)]
MASKED = -1e30
MIB = 2**20


def tp_ring(count):
    return list(range(0, count, 2)) + list(range(1, count, 2))[::-1]


def after(value, *gates):
    if not gates:
        return value
    return lax.optimization_barrier((value, gates))[0]


def norm_kernel(place_ref, x_ref, gain_ref, keep_ref, give_ref, far_ref, cross_ref):
    wide = x_ref[0].astype(jnp.float32)
    factor = lax.rsqrt(jnp.mean(wide * wide, axis=1, keepdims=True) + EPS)
    width = keep_ref.shape[1]
    req, kv = place_ref[0], place_ref[1]
    to = (2 * req + kv, 2 * req + 1 - kv, 2 - 2 * req + kv, 3 - 2 * req - kv)
    for quarter, ref in zip(to, (keep_ref, give_ref, far_ref, cross_ref)):
        at = pl.multiple_of(quarter * width, width)
        part = x_ref[0, :, pl.ds(at, width)].astype(jnp.float32)
        gain = gain_ref[:, pl.ds(at, width)].astype(jnp.float32)
        ref[...] = (part * factor * gain).astype(ref.dtype)


def norm(place, tokens, gain):
    rows, depth = tokens.shape[1:]
    whole = pl.BlockSpec(memory_space=pltpu.VMEM)
    quarter = jax.ShapeDtypeStruct((rows, depth // 4), jnp.bfloat16)
    return pl.pallas_call(
        norm_kernel,
        in_specs=[pl.BlockSpec(memory_space=pltpu.SMEM), whole, whole],
        out_specs=[whole] * 4,
        out_shape=[quarter] * 4,
        compiler_params=pltpu.CompilerParams(vmem_limit_bytes=4 * MIB),
        name="norm",
    )(place, tokens, gain.reshape(1, depth))


def load_kernel(count, *refs):
    copies = [
        pltpu.make_async_copy(source, to, refs[-1].at[number])
        for number, (source, to) in enumerate(zip(refs[:count], refs[count:]))
    ]
    for copy in copies:
        copy.start()
    for copy in copies:
        copy.wait()


def load(limit, *arrays):
    count = len(arrays)
    return pl.pallas_call(
        functools.partial(load_kernel, count),
        in_specs=[pl.BlockSpec(memory_space=pl.ANY)] * count,
        out_specs=[pl.BlockSpec(memory_space=pltpu.VMEM)] * count,
        out_shape=[pltpu.VMEM(a.shape, a.dtype) for a in arrays],
        scratch_shapes=[pltpu.SemaphoreType.DMA((count,))],
        compiler_params=pltpu.CompilerParams(vmem_limit_bytes=limit * MIB),
        name="load",
    )(*arrays)


def heads_kernel(place_ref, k_ref, v_ref, mine_ref, give_ref, sems):
    head_dim = mine_ref.shape[-1]
    kv, tp = place_ref[1], place_ref[2]
    copies = []
    for number, (out, core) in enumerate(((mine_ref, kv), (give_ref, 1 - kv))):
        at = pl.multiple_of((2 * tp + core) * head_dim, head_dim)
        for which, ref in enumerate((k_ref, v_ref)):
            copies.append(
                pltpu.make_async_copy(
                    ref.at[:, :, pl.ds(at, head_dim)], out.at[which], sems.at[2 * number + which]
                )
            )
    for copy in copies:
        copy.start()
    for copy in copies:
        copy.wait()


def cached_heads(place, keys, values):
    blocks, length = keys.shape[:2]
    out = jax.ShapeDtypeStruct((2, blocks, length, HD), keys.dtype)
    return pl.pallas_call(
        heads_kernel,
        in_specs=[pl.BlockSpec(memory_space=pltpu.SMEM)]
        + [pl.BlockSpec(memory_space=pl.ANY)] * 2,
        out_specs=[pl.BlockSpec(memory_space=pltpu.VMEM)] * 2,
        out_shape=[out] * 2,
        scratch_shapes=[pltpu.SemaphoreType.DMA((4,))],
        compiler_params=pltpu.CompilerParams(vmem_limit_bytes=4 * MIB),
        name="cached_heads",
    )(place, keys, values)


def merge_kernel(place_ref, mine_ref, theirs_ref, out_ref):
    rows = mine_ref.shape[0]
    kv = place_ref[1]
    out_ref[pl.ds(pl.multiple_of(kv * rows, rows), rows), :] = mine_ref[...]
    out_ref[pl.ds(pl.multiple_of((1 - kv) * rows, rows), rows), :] = theirs_ref[...]


def merge(place, mine, theirs):
    rows, columns = mine.shape
    whole = pl.BlockSpec(memory_space=pltpu.VMEM)
    return pl.pallas_call(
        merge_kernel,
        in_specs=[pl.BlockSpec(memory_space=pltpu.SMEM)] + [whole] * 2,
        out_specs=whole,
        out_shape=jax.ShapeDtypeStruct((2 * rows, columns), mine.dtype),
        compiler_params=pltpu.CompilerParams(vmem_limit_bytes=4 * MIB),
        name="merge",
    )(place, mine, theirs)


def share_kernel(place_ref, *refs):
    terms, (mine_ref, give_ref) = refs[:-2], refs[-2:]
    rows = mine_ref.shape[0]
    kv = place_ref[1]
    for core, ref in ((kv, mine_ref), (1 - kv, give_ref)):
        at = pl.ds(pl.multiple_of(core * rows, rows), rows)
        total = sum(term[at, :].astype(jnp.float32) for term in terms)
        ref[...] = total.astype(ref.dtype)


def share(place, *terms):
    rows, columns = terms[0].shape
    whole = pl.BlockSpec(memory_space=pltpu.VMEM)
    return pl.pallas_call(
        share_kernel,
        in_specs=[pl.BlockSpec(memory_space=pltpu.SMEM)] + [whole] * len(terms),
        out_specs=[whole] * 2,
        out_shape=[jax.ShapeDtypeStruct((rows // 2, columns), terms[0].dtype)] * 2,
        compiler_params=pltpu.CompilerParams(vmem_limit_bytes=4 * MIB),
        name="share",
    )(place, *terms)


def collect_kernel(place_ref, *refs):
    terms, out_ref = refs[:-1], refs[-1]
    width = terms[0].shape[1]
    req, kv = place_ref[0], place_ref[1]
    of = (2 * req + kv, 2 * req + 1 - kv, 2 - 2 * req + kv, 3 - 2 * req - kv)
    pairs = (terms[:1], terms[1:2], terms[2:4], terms[4:])
    for quarter, pair in zip(of, pairs):
        total = sum(term[...].astype(jnp.float32) for term in pair)
        at = pl.ds(pl.multiple_of(quarter * width, width), width)
        out_ref[0, :, at] = total.astype(out_ref.dtype)


def collect(place, mine, theirs, same, cross):
    rows, columns = mine.shape
    whole = pl.BlockSpec(memory_space=pltpu.VMEM)
    return pl.pallas_call(
        collect_kernel,
        in_specs=[pl.BlockSpec(memory_space=pltpu.SMEM)] + [whole] * 6,
        out_specs=whole,
        out_shape=jax.ShapeDtypeStruct((1, rows, 4 * columns), mine.dtype),
        compiler_params=pltpu.CompilerParams(vmem_limit_bytes=4 * MIB),
        name="collect",
    )(place, mine, theirs, *same, *cross)


def project_kernel(flips, place_ref, *refs):
    outputs = len(flips)
    pieces = refs[: -3 - outputs]
    q_ref, k_ref, v_ref = refs[-3 - outputs : -outputs]
    outs = refs[-outputs:]
    x = jnp.concatenate([piece[...] for piece in pieces], axis=0)
    head_dim = k_ref.shape[1] // 2
    width = 256
    base = q_ref.shape[1] // 2
    for number, out in enumerate(outs):
        kv = place_ref[1]
        half = 1 - kv if flips[number] else kv
        for t in range(base // width):
            at = pl.multiple_of(half * base + t * width, width)
            product = jnp.dot(x, q_ref[:, pl.ds(at, width)], preferred_element_type=jnp.float32)
            out[:, t * width : (t + 1) * width] = product.astype(out.dtype)
        at = pl.ds(pl.multiple_of(half * head_dim, head_dim), head_dim)
        both = jnp.concatenate((k_ref[:, at], v_ref[:, at]), axis=1)
        product = jnp.dot(x, both, preferred_element_type=jnp.float32)
        out[:, base:] = product.astype(out.dtype)


def project(place, pieces, weights, flips, kinds):
    rows = sum(piece.shape[0] for piece in pieces)
    total = sum(w.shape[1] for w in weights) // 2
    whole = pl.BlockSpec(memory_space=pltpu.VMEM)
    return pl.pallas_call(
        functools.partial(project_kernel, flips),
        in_specs=[pl.BlockSpec(memory_space=pltpu.SMEM)] + [whole] * (len(pieces) + 3),
        out_specs=[whole] * len(kinds),
        out_shape=[jax.ShapeDtypeStruct((rows, total), kind) for kind in kinds],
        compiler_params=pltpu.CompilerParams(vmem_limit_bytes=6 * MIB),
        name="project",
    )(place, *pieces, *weights)


def out_kernel(place_ref, own_ref, other_ref, w_ref, *outs):
    depth = own_ref.shape[1]
    part = own_ref.shape[0] // len(outs)
    mine = place_ref[1]
    at = pl.multiple_of(mine * depth, depth)
    off = pl.multiple_of((1 - mine) * depth, depth)
    own, other = own_ref[...], other_ref[...]
    width = 256
    for t in range(w_ref.shape[1] // width):
        columns = slice(t * width, (t + 1) * width)
        product = jnp.dot(
            own, w_ref[pl.ds(at, depth), columns], preferred_element_type=jnp.float32
        )
        product += jnp.dot(
            other, w_ref[pl.ds(off, depth), columns], preferred_element_type=jnp.float32
        )
        product = product.astype(outs[0].dtype)
        for j, out in enumerate(outs):
            out[:, columns] = product[j * part : (j + 1) * part]


def out_project(place, own, other, w_out, pieces):
    rows = own.shape[0]
    columns = w_out.shape[1]
    whole = pl.BlockSpec(memory_space=pltpu.VMEM)
    return pl.pallas_call(
        out_kernel,
        in_specs=[pl.BlockSpec(memory_space=pltpu.SMEM)] + [whole] * 3,
        out_specs=[whole] * pieces,
        out_shape=[jax.ShapeDtypeStruct((rows // pieces, columns), jnp.bfloat16)] * pieces,
        compiler_params=pltpu.CompilerParams(vmem_limit_bytes=6 * MIB),
        name="out_project",
    )(place, own, other, w_out)


def attend_kernel(wanted, order, parts, place_ref, ids_ref, seg_ref, *refs):
    keep_refs, come_refs = refs[:parts], refs[parts:-3]
    chip_ref, away_ref, out_ref = refs[-3:]
    req, kv, tp = place_ref[0], place_ref[1], place_ref[2]
    groups = 2
    steps = ids_ref.shape[1]
    total_cols = keep_refs[0].shape[1]
    rows = sum(ref.shape[0] for ref in keep_refs) // groups
    part = out_ref.shape[0] // (groups * len(wanted))
    pieces = rows // part
    some = part * len(wanted)
    head_dim = chip_ref.shape[-1]
    blocks, length = chip_ref.shape[2:4]
    heads = total_cols // head_dim - 2
    q_cols = heads * head_dim
    scale = head_dim**-0.5
    stack = min(heads, max(1, 256 // some))
    chain = CHAIN_BLOCKS * length

    def looked_up(index, options):
        result = jnp.int32(options[0])
        for number, option in enumerate(options[1:], 1):
            result = jnp.where(index == number, jnp.int32(option), result)
        return result

    spot = looked_up(tp, [order.index(i) for i in range(pieces)])
    source = [looked_up(lax.rem(spot - j + pieces, pieces), order) for j in range(pieces)]

    def branch(block, which):
        device = block // blocks
        near = device // 2 == req
        core = jnp.where(lax.rem(device, 2) == kv, 0, 1)
        at = lax.rem(block, blocks)
        here = chip_ref[core, which, pl.ds(at, CHAIN_BLOCKS)]
        there = away_ref[core, which, pl.ds(at, CHAIN_BLOCKS)]
        return jnp.where(near, here, there).reshape(chain, head_dim)

    def position(index, sources):
        piece = index // part
        start = jnp.full(index.shape, source[sources[0]], jnp.int32)
        for j in range(1, len(sources)):
            start = jnp.where(piece == j, source[sources[j]], start)
        return start * part + index % part

    row_pos = position(lax.broadcasted_iota(jnp.int32, (some, rows), 0), wanted)
    across = lax.broadcasted_iota(jnp.int32, (some, rows), 1)
    col_pos = position(across, range(pieces))
    keep = jnp.concatenate([ref[...] for ref in keep_refs], axis=0)
    come = jnp.concatenate([ref[...] for ref in come_refs], axis=0)
    whole = (keep + come.astype(jnp.float32)).astype(jnp.bfloat16)

    def own_rows(g, j, columns):
        at = (j * groups + g) * part
        return whole[at : at + part, columns]

    for g in range(groups):
        group = 2 * req + g
        segments = seg_ref[pl.ds(group, 1), :]
        root = jnp.int32(0)
        keys, values = [branch(root, 0)], [branch(root, 1)]
        bias = [jnp.zeros((some, chain), jnp.float32)]
        same = None
        low = jnp.int32(0)
        for s in range(steps):
            first = ids_ref[group, s, ROOT_BLOCKS]
            count = jnp.int32(0)
            for slot in range(CHAIN_BLOCKS):
                count += jnp.where(ids_ref[group, s, ROOT_BLOCKS + slot] >= 0, length, 0)
            high = jnp.sum((segments <= s).astype(jnp.int32))
            keys.append(branch(first, 0))
            values.append(branch(first, 1))
            row_in = (row_pos >= low) & (row_pos < high)
            col_in = (col_pos >= low) & (col_pos < high)
            both = row_in & col_in
            same = both if same is None else same | both
            for piece in range(chain // rows):
                allowed = row_in & (across + piece * rows < count)
                bias.append(jnp.where(allowed, 0.0, MASKED))
            low = high
        for j in range(pieces):
            keys.append(own_rows(g, j, slice(q_cols, q_cols + head_dim)))
            values.append(own_rows(g, j, slice(q_cols + head_dim, None)))
        bias.append(jnp.where(same & (col_pos <= row_pos), 0.0, MASKED))
        keys = jnp.concatenate(keys, axis=0)
        values = jnp.concatenate(values, axis=0)
        bias = jnp.concatenate(bias, axis=1)
        bias = jnp.concatenate([bias] * stack, axis=0)
        for low_head in range(0, heads, stack):
            query = jnp.concatenate(
                [
                    own_rows(g, j, slice(h * head_dim, (h + 1) * head_dim))
                    for h in range(low_head, low_head + stack)
                    for j in wanted
                ],
                axis=0,
            )
            scores = lax.dot_general(
                query, keys, (((1,), (1,)), ((), ())), preferred_element_type=jnp.float32
            )
            scores = scores * scale + bias
            top = jnp.max(scores, axis=1, keepdims=True)
            weights = jnp.exp(scores - top)
            total = jnp.sum(weights, axis=1, keepdims=True)
            summed = jnp.dot(
                weights.astype(jnp.bfloat16), values, preferred_element_type=jnp.float32
            )
            result = (summed / total).astype(out_ref.dtype)
            for n in range(stack):
                columns = slice((low_head + n) * head_dim, (low_head + n + 1) * head_dim)
                for number in range(len(wanted)):
                    of, to = n * some + number * part, (number * groups + g) * part
                    out_ref[to : to + part, columns] = result[of : of + part]


def attend(wanted, order, place, ids, segments, keep, come, chip, away, part):
    rows = 2 * len(wanted) * part
    whole = pl.BlockSpec(memory_space=pltpu.VMEM)
    scalars = pl.BlockSpec(memory_space=pltpu.SMEM)
    return pl.pallas_call(
        functools.partial(attend_kernel, wanted, order, len(keep)),
        in_specs=[scalars] * 2 + [whole] * (len(keep) + len(come) + 3),
        out_specs=whole,
        out_shape=jax.ShapeDtypeStruct((rows, keep[0].shape[1] - 2 * HD), jnp.bfloat16),
        compiler_params=pltpu.CompilerParams(vmem_limit_bytes=10 * MIB),
        name="attend",
    )(place, ids, segments, *keep, *come, chip, away)


ROOT_BLOCKS = 4
CHAIN_BLOCKS = 4


def on_device(
    tokens, norm_gain, w_query, w_key, w_value, w_out, cache_keys, cache_values, seg_ids, block_ids
):
    req, kv, tp = lax.axis_index("req"), lax.axis_index("kv"), lax.axis_index("tp")
    part = tokens.shape[1]
    count = lax.axis_size("tp")
    order = tp_ring(count)
    forward = [(order[i], order[(i + 1) % count]) for i in range(count)]
    place = jnp.stack((req, kv, tp)).astype(jnp.int32)

    def swap_req(x):
        return lax.ppermute(x, "req", SWAP)

    def swap_kv(x):
        return lax.ppermute(x, "kv", SWAP)

    def swap_both(x):
        return lax.ppermute(x, ("req", "kv"), [(i, 3 - i) for i in range(4)])

    def onward(x):
        return lax.ppermute(x, "tp", forward)

    def slanted(same, cross):
        axes = ("tp", "req", "kv")
        return [
            lax.ppermute(
                x,
                axes,
                [
                    (4 * low + 2 * r + c, 4 * high + 2 * (1 - r) + (c ^ flip))
                    for low, high in forward
                    for r in range(2)
                    for c in range(2)
                ],
            )
            for flip, x in enumerate((same, cross))
        ]

    kept, give, far_same, far_cross = norm(place, tokens, norm_gain)
    near = merge(place, kept, swap_kv(give))
    far = merge(place, swap_req(far_same), swap_both(far_cross))

    kinds = (jnp.bfloat16, jnp.float32)

    def summed(sent, kept, kind):
        return (kept + swap_kv(sent).astype(jnp.float32)).astype(kind)

    near_pieces, far_pieces = [near, onward(near)], [far]
    weights = load(46, *after((w_query, w_key, w_value), near))
    far_pieces.append(onward(after(far, weights)))
    mine, give = cached_heads(place, *after((cache_keys, cache_values), weights))
    chip = jnp.stack((mine, swap_kv(give)))
    away = swap_req(chip)
    far_first = project(place, far_pieces, weights, (True, False), kinds)
    for step in range(1, count - 1):
        piece = near_pieces[step]
        near_pieces.append(onward(after(piece, far_first) if step == count - 2 else piece))
        far_pieces.append(onward(far_pieces[step]))
    first_terms = summed(*far_first, jnp.bfloat16)

    near_terms = project(place, after(near_pieces, away), weights, (True, False), kinds)
    keep = (summed(*near_terms, jnp.float32),)
    pieces = after(far_pieces[2:], near_terms)
    sent = project(place, pieces, weights, (True,), kinds[:1])
    kept = project(place, pieces, weights, (False,), kinds[1:])
    last_terms = summed(*sent, *kept, jnp.bfloat16)
    come = (swap_req(first_terms), swap_req(last_terms))
    w_out = load(38, *after((w_out,), last_terms))[0]

    middle = count // 2
    halves = (tuple(range(1, middle + 1)), tuple(j % count for j in range(middle + 1, count + 1)))
    near_sum, far_sum = {}, {}

    def attended(wanted, *gates):
        inputs = after(keep, *gates)
        return attend(
            wanted, order, place, block_ids, seg_ids, inputs, come, chip, away, part
        )

    def projected(sums, wanted, own, other):
        sums |= zip(wanted, out_project(place, own, other, w_out, len(wanted)))

    def plus(running, term):
        return (running.astype(jnp.float32) + term.astype(jnp.float32)).astype(jnp.bfloat16)

    rows = attended(halves[0], w_out)
    rows_far = swap_req(rows)
    projected(near_sum, halves[0], rows, swap_kv(rows))
    near_run = near_one = onward(near_sum[1])
    last = attended(halves[1], near_sum[1])
    last_far = swap_req(last)
    rows_far = after(rows_far, last)
    rows_far = after((rows_far, swap_kv(rows_far)), last)
    projected(far_sum, halves[0], *rows_far)
    far_run = onward(far_sum[1])
    projected(near_sum, halves[1], last, swap_kv(last))
    last_far = after(last_far, near_one)
    projected(far_sum, halves[1], last_far, swap_kv(last_far))

    terms = share(place, after(far_sum[0], far_run))
    beside = (swap_req(terms[0]), swap_both(terms[1]))
    for j in range(2, count):
        near_term = plus(near_run, near_sum[j])
        near_run = onward(after(near_term, terms) if j == count - 1 else near_term)
        if j < count - 1:
            far_run = onward(plus(far_run, far_sum[j]))
    ends = slanted(*share(place, far_run, far_sum[count - 1]))
    mine, give = share(place, near_run, near_sum[0])
    return collect(place, mine, swap_kv(give), *zip(ends, beside))


def fits(shape):
    local_kv = KVH // shape["tp"]
    return shape["req"] == 2 and shape["kv"] == 2 and shape["tp"] > 1 and local_kv == 2


def solution(mesh):
    placed = (
        P(("grp", "req", "kv"), "tp", None),
        P(),
        P(("req", "kv"), "tp"),
        P(("req", "kv"), "tp"),
        P(("req", "kv"), "tp"),
        P("tp", ("req", "kv")),
        P(("grp", "req", "kv"), None, None),
        P(("grp", "req", "kv"), None, None),
        P("grp", None),
        P("grp", None, None),
    )
    return jax.shard_map(
        on_device if fits(mesh.shape) else general_path,
        mesh=mesh,
        in_specs=placed,
        out_specs=P(("grp", "req", "kv"), "tp", None),
        check_vma=False,
    )
```

```python
import functools

import jax
import jax.numpy as jnp
from jax import lax
from jax.experimental import pallas as pl
from jax.experimental.pallas import tpu as pltpu
from jax.sharding import PartitionSpec as P

HQ = 64
KVH = 8
HD = 128


EPS = 1e-06


def swapped(block, axis, distance):
    count = lax.axis_size(axis)
    route = []
    for low in range(count):
        high = low | 1 << distance
        if high != low and high < count:
            route += [(low, high), (high, low)]
    return lax.ppermute(block, axis, route)


def combined_all(shard, axis, join):
    gathered = jax.tree.map(
        lambda a, kind: lax.all_gather(a.astype(kind), axis),
        shard,
        jax.tree.map(lambda a: jnp.bfloat16 if a.dtype == jnp.float32 else a.dtype, shard),
    )

    def take(source):
        return jax.tree.map(
            lambda a, own: lax.dynamic_index_in_dim(a, source, 0, False).astype(own.dtype),
            gathered,
            shard,
        )

    return lax.fori_loop(
        1, lax.axis_size(axis), lambda source, state: join(state, take(source)), take(0)
    )


def partial_attend(heads, keys, values, allowed, scale):
    scores = jnp.einsum("rkgd,nkd->rkgn", heads, keys, preferred_element_type=jnp.float32) * scale
    wide_mask = allowed[:, None, None, :]
    scores = jnp.where(wide_mask, scores, -1e30)
    top = jnp.max(scores, axis=-1)
    weights = jnp.where(wide_mask, jnp.exp(scores - top[..., None]), 0.0)
    total = jnp.sum(weights, axis=-1)
    summed = jnp.einsum(
        "rkgn,nkd->rkgd", weights.astype(jnp.bfloat16), values, preferred_element_type=jnp.float32
    )
    return (top, total, summed)


def combine(first, second):
    top = jnp.maximum(first[0], second[0])
    left = jnp.exp(first[0] - top)
    right = jnp.exp(second[0] - top)
    return (
        top,
        first[1] * left + second[1] * right,
        first[2] * left[..., None] + second[2] * right[..., None],
    )


def general_path(
    tokens, norm_gain, w_query, w_key, w_value, w_out, cache_keys, cache_values, seg_ids, block_ids
):
    groups = seg_ids.shape[0]
    rows = seg_ids.shape[1]
    steps = block_ids.shape[1]
    group = lax.axis_index(("req", "kv"))
    tp_index = lax.axis_index("tp")
    head_dim = HD
    gsize = HQ // KVH
    local_heads = w_query.shape[1] // head_dim
    per_kv = min(gsize, local_heads)
    kv_count = local_heads // per_kv
    first_kv = tp_index * local_heads // gsize
    scale = head_dim ** (-0.5)
    blocks_here = cache_keys.shape[0]
    block_len = cache_keys.shape[1]
    blocks_all = blocks_here * groups
    wide = tokens[0].astype(jnp.float32)
    normed = (
        wide
        * lax.rsqrt(jnp.mean(wide * wide, axis=-1, keepdims=True) + EPS)
        * norm_gain.astype(jnp.float32)
    ).astype(jnp.bfloat16)
    whole = lax.all_gather(normed, "tp", axis=0, tiled=True)
    pieces = (
        lax.all_gather(w_query, ("req", "kv"), axis=0, tiled=True),
        lax.all_gather(w_key, ("req", "kv"), axis=0, tiled=True),
        lax.all_gather(w_value, ("req", "kv"), axis=0, tiled=True),
    )
    query_acc, key_acc, value_acc = tuple(
        (jnp.dot(whole, piece, preferred_element_type=jnp.float32) for piece in pieces)
    )
    queries = query_acc.astype(jnp.bfloat16)
    span = max(1, gsize // local_heads)
    stacked = jnp.stack((key_acc.astype(jnp.bfloat16), value_acc.astype(jnp.bfloat16)))
    for bit in range(span.bit_length() - 1):
        partner = swapped(stacked, "tp", bit)
        upper = tp_index // (1 << bit) % 2 == 1
        stacked = jnp.where(
            upper, jnp.concatenate((partner, stacked), 2), jnp.concatenate((stacked, partner), 2)
        )
    own_keys = stacked[0].reshape(rows, kv_count, head_dim)
    own_values = stacked[1].reshape(rows, kv_count, head_dim)
    heads = queries.reshape(rows, kv_count, per_kv, head_dim)
    member = jnp.any(
        block_ids[..., None] == jnp.arange(blocks_all, dtype=jnp.int32), axis=-2
    ).astype(jnp.float32)
    onehot = (seg_ids[..., None] == jnp.arange(steps, dtype=jnp.int32)).astype(jnp.float32)
    block_mask = jnp.einsum("grs,gsb->grb", onehot, member) > 0.5
    seg_here = lax.dynamic_index_in_dim(seg_ids, group, 0, keepdims=False)
    places = jnp.arange(rows, dtype=jnp.int32)
    own_mask = (seg_here[:, None] == seg_here[None, :]) & (places[:, None] >= places[None, :])
    own_part = partial_attend(heads, own_keys, own_values, own_mask, scale)
    gathered = lax.all_gather(queries[None], ("req", "kv"), axis=0, tiled=True)
    all_heads = gathered.reshape(groups * rows, kv_count, per_kv, head_dim)
    local_keys = lax.dynamic_slice_in_dim(
        cache_keys, first_kv * head_dim, kv_count * head_dim, 2
    ).reshape(blocks_here * block_len, kv_count, head_dim)
    local_values = lax.dynamic_slice_in_dim(
        cache_values, first_kv * head_dim, kv_count * head_dim, 2
    ).reshape(blocks_here * block_len, kv_count, head_dim)
    local_blocks = lax.dynamic_slice_in_dim(
        block_mask, group * blocks_here, blocks_here, 2
    ).reshape(groups * rows, blocks_here)
    local_mask = jnp.repeat(local_blocks, block_len, axis=1)
    cache_part = partial_attend(all_heads, local_keys, local_values, local_mask, scale)
    merged = combined_all(cache_part, ("req", "kv"), combine)
    mine = tuple((lax.dynamic_slice_in_dim(item, group * rows, rows, 0) for item in merged))
    top, total, summed = combine(mine, own_part)
    attended = (
        (summed / total[..., None]).astype(jnp.bfloat16).reshape(rows, local_heads * head_dim)
    )
    out_full = lax.all_gather(w_out, ("req", "kv"), axis=1, tiled=True)
    branch = lax.psum_scatter(
        jnp.dot(attended, out_full, preferred_element_type=jnp.float32).astype(jnp.bfloat16),
        "tp",
        scatter_dimension=0,
        tiled=True,
    )
    return branch[None]


SWAP = [(0, 1), (1, 0)]
MASKED = -1e30
MIB = 2**20


def tp_ring(count):
    return list(range(0, count, 2)) + list(range(1, count, 2))[::-1]


def after(value, *gates):
    if not gates:
        return value
    return lax.optimization_barrier((value, gates))[0]


def norm_kernel(place_ref, x_ref, gain_ref, keep_ref, give_ref, far_ref, cross_ref):
    wide = x_ref[0].astype(jnp.float32)
    factor = lax.rsqrt(jnp.mean(wide * wide, axis=1, keepdims=True) + EPS)
    width = keep_ref.shape[1]
    req, kv = place_ref[0], place_ref[1]
    to = (2 * req + kv, 2 * req + 1 - kv, 2 - 2 * req + kv, 3 - 2 * req - kv)
    for quarter, ref in zip(to, (keep_ref, give_ref, far_ref, cross_ref)):
        at = pl.multiple_of(quarter * width, width)
        part = x_ref[0, :, pl.ds(at, width)].astype(jnp.float32)
        gain = gain_ref[:, pl.ds(at, width)].astype(jnp.float32)
        ref[...] = (part * factor * gain).astype(ref.dtype)


def norm(place, tokens, gain):
    rows, depth = tokens.shape[1:]
    whole = pl.BlockSpec(memory_space=pltpu.VMEM)
    quarter = jax.ShapeDtypeStruct((rows, depth // 4), jnp.bfloat16)
    return pl.pallas_call(
        norm_kernel,
        in_specs=[pl.BlockSpec(memory_space=pltpu.SMEM), whole, whole],
        out_specs=[whole] * 4,
        out_shape=[quarter] * 4,
        compiler_params=pltpu.CompilerParams(vmem_limit_bytes=4 * MIB),
        name="norm",
    )(place, tokens, gain.reshape(1, depth))


def load_kernel(count, *refs):
    copies = [
        pltpu.make_async_copy(source, to, refs[-1].at[number])
        for number, (source, to) in enumerate(zip(refs[:count], refs[count:]))
    ]
    for copy in copies:
        copy.start()
    for copy in copies:
        copy.wait()


def load(limit, *arrays):
    count = len(arrays)
    return pl.pallas_call(
        functools.partial(load_kernel, count),
        in_specs=[pl.BlockSpec(memory_space=pl.ANY)] * count,
        out_specs=[pl.BlockSpec(memory_space=pltpu.VMEM)] * count,
        out_shape=[pltpu.VMEM(a.shape, a.dtype) for a in arrays],
        scratch_shapes=[pltpu.SemaphoreType.DMA((count,))],
        compiler_params=pltpu.CompilerParams(vmem_limit_bytes=limit * MIB),
        name="load",
    )(*arrays)


def heads_kernel(place_ref, k_ref, v_ref, mine_ref, give_ref, sems):
    head_dim = mine_ref.shape[-1]
    kv, tp = place_ref[1], place_ref[2]
    copies = []
    for number, (out, core) in enumerate(((mine_ref, kv), (give_ref, 1 - kv))):
        at = pl.multiple_of((2 * tp + core) * head_dim, head_dim)
        for which, ref in enumerate((k_ref, v_ref)):
            copies.append(
                pltpu.make_async_copy(
                    ref.at[:, :, pl.ds(at, head_dim)], out.at[which], sems.at[2 * number + which]
                )
            )
    for copy in copies:
        copy.start()
    for copy in copies:
        copy.wait()


def cached_heads(place, keys, values):
    blocks, length = keys.shape[:2]
    out = jax.ShapeDtypeStruct((2, blocks, length, HD), keys.dtype)
    return pl.pallas_call(
        heads_kernel,
        in_specs=[pl.BlockSpec(memory_space=pltpu.SMEM)]
        + [pl.BlockSpec(memory_space=pl.ANY)] * 2,
        out_specs=[pl.BlockSpec(memory_space=pltpu.VMEM)] * 2,
        out_shape=[out] * 2,
        scratch_shapes=[pltpu.SemaphoreType.DMA((4,))],
        compiler_params=pltpu.CompilerParams(vmem_limit_bytes=4 * MIB),
        name="cached_heads",
    )(place, keys, values)


def collect_kernel(place_ref, *refs):
    terms, out_ref = refs[:-1], refs[-1]
    width = terms[0].shape[1]
    req, kv = place_ref[0], place_ref[1]
    of = (2 * req + kv, 2 * req + 1 - kv, 2 - 2 * req + kv, 3 - 2 * req - kv)
    pairs = (terms[:1], terms[1:2], terms[2:4], terms[4:])
    for quarter, pair in zip(of, pairs):
        total = sum(term[...].astype(jnp.float32) for term in pair)
        at = pl.ds(pl.multiple_of(quarter * width, width), width)
        out_ref[0, :, at] = total.astype(out_ref.dtype)


def collect(place, mine, theirs, same, cross):
    rows, columns = mine.shape
    whole = pl.BlockSpec(memory_space=pltpu.VMEM)
    return pl.pallas_call(
        collect_kernel,
        in_specs=[pl.BlockSpec(memory_space=pltpu.SMEM)] + [whole] * 6,
        out_specs=whole,
        out_shape=jax.ShapeDtypeStruct((1, rows, 4 * columns), mine.dtype),
        compiler_params=pltpu.CompilerParams(vmem_limit_bytes=4 * MIB),
        name="collect",
    )(place, mine, theirs, *same, *cross)


def project_kernel(flips, place_ref, *refs):
    outputs = len(flips)
    pieces = refs[: -3 - outputs]
    q_ref, k_ref, v_ref = refs[-3 - outputs : -outputs]
    outs = refs[-outputs:]
    x = jnp.concatenate([piece[...] for piece in pieces], axis=0)
    head_dim = k_ref.shape[1] // 2
    width = 256
    base = q_ref.shape[1] // 2
    for number, out in enumerate(outs):
        kv = place_ref[1]
        half = 1 - kv if flips[number] else kv
        for t in range(base // width):
            at = pl.multiple_of(half * base + t * width, width)
            product = jnp.dot(x, q_ref[:, pl.ds(at, width)], preferred_element_type=jnp.float32)
            out[:, t * width : (t + 1) * width] = product.astype(out.dtype)
        at = pl.ds(pl.multiple_of(half * head_dim, head_dim), head_dim)
        both = jnp.concatenate((k_ref[:, at], v_ref[:, at]), axis=1)
        product = jnp.dot(x, both, preferred_element_type=jnp.float32)
        out[:, base:] = product.astype(out.dtype)


def project(place, pieces, weights, flips, kinds):
    rows = sum(piece.shape[0] for piece in pieces)
    total = sum(w.shape[1] for w in weights) // 2
    whole = pl.BlockSpec(memory_space=pltpu.VMEM)
    return pl.pallas_call(
        functools.partial(project_kernel, flips),
        in_specs=[pl.BlockSpec(memory_space=pltpu.SMEM)] + [whole] * (len(pieces) + 3),
        out_specs=[whole] * len(kinds),
        out_shape=[jax.ShapeDtypeStruct((rows, total), kind) for kind in kinds],
        compiler_params=pltpu.CompilerParams(vmem_limit_bytes=6 * MIB),
        name="project",
    )(place, *pieces, *weights)


def out_kernel(place_ref, own_ref, other_ref, w_ref, *outs):
    depth = own_ref.shape[1]
    part = own_ref.shape[0] // len(outs)
    mine = place_ref[1]
    at = pl.multiple_of(mine * depth, depth)
    off = pl.multiple_of((1 - mine) * depth, depth)
    own, other = own_ref[...], other_ref[...]
    width = 256
    for t in range(w_ref.shape[1] // width):
        columns = slice(t * width, (t + 1) * width)
        product = jnp.dot(
            own, w_ref[pl.ds(at, depth), columns], preferred_element_type=jnp.float32
        )
        product += jnp.dot(
            other, w_ref[pl.ds(off, depth), columns], preferred_element_type=jnp.float32
        )
        product = product.astype(outs[0].dtype)
        for j, out in enumerate(outs):
            out[:, columns] = product[j * part : (j + 1) * part]


def out_project(place, own, other, w_out, pieces):
    rows = own.shape[0]
    columns = w_out.shape[1]
    whole = pl.BlockSpec(memory_space=pltpu.VMEM)
    return pl.pallas_call(
        out_kernel,
        in_specs=[pl.BlockSpec(memory_space=pltpu.SMEM)] + [whole] * 3,
        out_specs=[whole] * pieces,
        out_shape=[jax.ShapeDtypeStruct((rows // pieces, columns), jnp.bfloat16)] * pieces,
        compiler_params=pltpu.CompilerParams(vmem_limit_bytes=6 * MIB),
        name="out_project",
    )(place, own, other, w_out)


def attend_kernel(wanted, order, parts, place_ref, ids_ref, seg_ref, *refs):
    keep_refs, come_refs = refs[:parts], refs[parts:-3]
    chip_ref, away_ref, out_ref = refs[-3:]
    req, kv, tp = place_ref[0], place_ref[1], place_ref[2]
    groups = 2
    steps = ids_ref.shape[1]
    total_cols = keep_refs[0].shape[1]
    rows = sum(ref.shape[0] for ref in keep_refs) // groups
    part = out_ref.shape[0] // (groups * len(wanted))
    pieces = rows // part
    some = part * len(wanted)
    head_dim = chip_ref.shape[-1]
    blocks, length = chip_ref.shape[2:4]
    heads = total_cols // head_dim - 2
    q_cols = heads * head_dim
    scale = head_dim**-0.5
    stack = min(heads, max(1, 256 // some))
    chain = CHAIN_BLOCKS * length

    def looked_up(index, options):
        result = jnp.int32(options[0])
        for number, option in enumerate(options[1:], 1):
            result = jnp.where(index == number, jnp.int32(option), result)
        return result

    spot = looked_up(tp, [order.index(i) for i in range(pieces)])
    source = [looked_up(lax.rem(spot - j + pieces, pieces), order) for j in range(pieces)]

    def branch(block, which):
        device = block // blocks
        near = device // 2 == req
        core = jnp.where(lax.rem(device, 2) == kv, 0, 1)
        at = lax.rem(block, blocks)
        here = chip_ref[core, which, pl.ds(at, CHAIN_BLOCKS)]
        there = away_ref[core, which, pl.ds(at, CHAIN_BLOCKS)]
        return jnp.where(near, here, there).reshape(chain, head_dim)

    def position(index, sources):
        piece = index // part
        start = jnp.full(index.shape, source[sources[0]], jnp.int32)
        for j in range(1, len(sources)):
            start = jnp.where(piece == j, source[sources[j]], start)
        return start * part + index % part

    row_pos = position(lax.broadcasted_iota(jnp.int32, (some, rows), 0), wanted)
    across = lax.broadcasted_iota(jnp.int32, (some, rows), 1)
    col_pos = position(across, range(pieces))
    keep = jnp.concatenate([ref[...] for ref in keep_refs], axis=0)
    come = jnp.concatenate([ref[...] for ref in come_refs], axis=0)
    whole = (keep + come.astype(jnp.float32)).astype(jnp.bfloat16)

    def own_rows(g, j, columns):
        at = (j * groups + g) * part
        return whole[at : at + part, columns]

    for g in range(groups):
        group = 2 * req + g
        segments = seg_ref[pl.ds(group, 1), :]
        root = jnp.int32(0)
        keys, values = [branch(root, 0)], [branch(root, 1)]
        bias = [jnp.zeros((some, chain), jnp.float32)]
        same = None
        low = jnp.int32(0)
        for s in range(steps):
            first = ids_ref[group, s, ROOT_BLOCKS]
            count = jnp.int32(0)
            for slot in range(CHAIN_BLOCKS):
                count += jnp.where(ids_ref[group, s, ROOT_BLOCKS + slot] >= 0, length, 0)
            high = jnp.sum((segments <= s).astype(jnp.int32))
            keys.append(branch(first, 0))
            values.append(branch(first, 1))
            row_in = (row_pos >= low) & (row_pos < high)
            col_in = (col_pos >= low) & (col_pos < high)
            both = row_in & col_in
            same = both if same is None else same | both
            for piece in range(chain // rows):
                allowed = row_in & (across + piece * rows < count)
                bias.append(jnp.where(allowed, 0.0, MASKED))
            low = high
        for j in range(pieces):
            keys.append(own_rows(g, j, slice(q_cols, q_cols + head_dim)))
            values.append(own_rows(g, j, slice(q_cols + head_dim, None)))
        bias.append(jnp.where(same & (col_pos <= row_pos), 0.0, MASKED))
        keys = jnp.concatenate(keys, axis=0)
        values = jnp.concatenate(values, axis=0)
        bias = jnp.concatenate(bias, axis=1)
        bias = jnp.concatenate([bias] * stack, axis=0)
        for low_head in range(0, heads, stack):
            query = jnp.concatenate(
                [
                    own_rows(g, j, slice(h * head_dim, (h + 1) * head_dim))
                    for h in range(low_head, low_head + stack)
                    for j in wanted
                ],
                axis=0,
            )
            scores = lax.dot_general(
                query, keys, (((1,), (1,)), ((), ())), preferred_element_type=jnp.float32
            )
            scores = scores * scale + bias
            top = jnp.max(scores, axis=1, keepdims=True)
            weights = jnp.exp(scores - top)
            total = jnp.sum(weights, axis=1, keepdims=True)
            summed = jnp.dot(
                weights.astype(jnp.bfloat16), values, preferred_element_type=jnp.float32
            )
            result = (summed / total).astype(out_ref.dtype)
            for n in range(stack):
                columns = slice((low_head + n) * head_dim, (low_head + n + 1) * head_dim)
                for number in range(len(wanted)):
                    of, to = n * some + number * part, (number * groups + g) * part
                    out_ref[to : to + part, columns] = result[of : of + part]


def attend(wanted, order, place, ids, segments, keep, come, chip, away, part):
    rows = 2 * len(wanted) * part
    whole = pl.BlockSpec(memory_space=pltpu.VMEM)
    scalars = pl.BlockSpec(memory_space=pltpu.SMEM)
    return pl.pallas_call(
        functools.partial(attend_kernel, wanted, order, len(keep)),
        in_specs=[scalars] * 2 + [whole] * (len(keep) + len(come) + 3),
        out_specs=whole,
        out_shape=jax.ShapeDtypeStruct((rows, keep[0].shape[1] - 2 * HD), jnp.bfloat16),
        compiler_params=pltpu.CompilerParams(vmem_limit_bytes=10 * MIB),
        name="attend",
    )(place, ids, segments, *keep, *come, chip, away)


ROOT_BLOCKS = 4
CHAIN_BLOCKS = 4


def on_device(
    tokens, norm_gain, w_query, w_key, w_value, w_out, cache_keys, cache_values, seg_ids, block_ids
):
    req, kv, tp = lax.axis_index("req"), lax.axis_index("kv"), lax.axis_index("tp")
    part = tokens.shape[1]
    count = lax.axis_size("tp")
    order = tp_ring(count)
    forward = [(order[i], order[(i + 1) % count]) for i in range(count)]
    place = jnp.stack((req, kv, tp)).astype(jnp.int32)

    def swap_req(x):
        return lax.ppermute(x, "req", SWAP)

    def swap_kv(x):
        return lax.ppermute(x, "kv", SWAP)

    def swap_both(x):
        return lax.ppermute(x, ("req", "kv"), [(i, 3 - i) for i in range(4)])

    def onward(x):
        return lax.ppermute(x, "tp", forward)

    def slanted(same, cross):
        axes = ("tp", "req", "kv")
        return [
            lax.ppermute(
                x,
                axes,
                [
                    (4 * low + 2 * r + c, 4 * high + 2 * (1 - r) + (c ^ flip))
                    for low, high in forward
                    for r in range(2)
                    for c in range(2)
                ],
            )
            for flip, x in enumerate((same, cross))
        ]

    first = kv == 0

    def merged(mine, theirs):
        return jnp.where(
            first, jnp.concatenate((mine, theirs)), jnp.concatenate((theirs, mine))
        )

    def shared(rows):
        low, high = rows[:part], rows[part:]
        return jnp.where(first, low, high), jnp.where(first, high, low)

    kept, give, far_same, far_cross = norm(place, tokens, norm_gain)
    near = merged(kept, swap_kv(give))
    far = merged(swap_req(far_same), swap_both(far_cross))

    kinds = (jnp.bfloat16, jnp.float32)

    def summed(sent, kept, kind):
        return (kept + swap_kv(sent).astype(jnp.float32)).astype(kind)

    near_pieces, far_pieces = [near, onward(near)], [far]
    weights = load(46, *after((w_query, w_key, w_value), near))
    far_pieces.append(onward(after(far, weights)))
    mine, give = cached_heads(place, *after((cache_keys, cache_values), weights))
    chip = jnp.stack((mine, swap_kv(give)))
    away = swap_req(chip)
    far_first = project(place, far_pieces, weights, (True, False), kinds)
    for step in range(1, count - 1):
        piece = near_pieces[step]
        near_pieces.append(onward(after(piece, far_first) if step == count - 2 else piece))
        far_pieces.append(onward(far_pieces[step]))
    first_terms = summed(*far_first, jnp.bfloat16)

    near_terms = project(place, after(near_pieces, away), weights, (True, False), kinds)
    keep = (summed(*near_terms, jnp.float32),)
    pieces = after(far_pieces[2:], near_terms)
    sent = project(place, pieces, weights, (True,), kinds[:1])
    kept = project(place, pieces, weights, (False,), kinds[1:])
    last_terms = summed(*sent, *kept, jnp.bfloat16)
    come = (swap_req(first_terms), swap_req(last_terms))
    w_out = load(38, *after((w_out,), last_terms))[0]

    middle = count // 2
    halves = (tuple(range(1, middle + 1)), tuple(j % count for j in range(middle + 1, count + 1)))
    near_sum, far_sum = {}, {}

    def attended(wanted, *gates):
        inputs = after(keep, *gates)
        return attend(
            wanted, order, place, block_ids, seg_ids, inputs, come, chip, away, part
        )

    def projected(sums, wanted, own, other):
        sums |= zip(wanted, out_project(place, own, other, w_out, len(wanted)))

    def plus(running, term):
        return (running.astype(jnp.float32) + term.astype(jnp.float32)).astype(jnp.bfloat16)

    rows = attended(halves[0], w_out)
    rows_far = swap_req(rows)
    projected(near_sum, halves[0], rows, swap_kv(rows))
    near_run = near_one = onward(near_sum[1])
    last = attended(halves[1], near_sum[1])
    last_far = swap_req(last)
    rows_far = after(rows_far, last)
    rows_far = after((rows_far, swap_kv(rows_far)), last)
    projected(far_sum, halves[0], *rows_far)
    far_run = onward(far_sum[1])
    projected(near_sum, halves[1], last, swap_kv(last))
    last_far = after(last_far, near_one)
    projected(far_sum, halves[1], last_far, swap_kv(last_far))

    terms = shared(after(far_sum[0], far_run))
    beside = (swap_req(terms[0]), swap_both(terms[1]))
    for j in range(2, count):
        near_term = plus(near_run, near_sum[j])
        near_run = onward(after(near_term, terms) if j == count - 1 else near_term)
        if j < count - 1:
            far_run = onward(plus(far_run, far_sum[j]))
    ends = slanted(*shared(plus(far_run, far_sum[count - 1])))
    mine, give = shared(plus(near_run, near_sum[0]))
    return collect(place, mine, swap_kv(give), *zip(ends, beside))


def fits(shape):
    local_kv = KVH // shape["tp"]
    return shape["req"] == 2 and shape["kv"] == 2 and shape["tp"] > 1 and local_kv == 2


def solution(mesh):
    placed = (
        P(("grp", "req", "kv"), "tp", None),
        P(),
        P(("req", "kv"), "tp"),
        P(("req", "kv"), "tp"),
        P(("req", "kv"), "tp"),
        P("tp", ("req", "kv")),
        P(("grp", "req", "kv"), None, None),
        P(("grp", "req", "kv"), None, None),
        P("grp", None),
        P("grp", None, None),
    )
    return jax.shard_map(
        on_device if fits(mesh.shape) else general_path,
        mesh=mesh,
        in_specs=placed,
        out_specs=P(("grp", "req", "kv"), "tp", None),
        check_vma=False,
    )
```

```python
import functools
import math

import jax
import jax.numpy as jnp
from jax import lax
from jax.experimental import pallas as pl
from jax.experimental.pallas import tpu as pltpu
from jax.sharding import PartitionSpec as P

HQ = 64
KVH = 8
HD = 128


EPS = 1e-06


def swapped(block, axis, distance):
    count = lax.axis_size(axis)
    route = []
    for low in range(count):
        high = low | 1 << distance
        if high != low and high < count:
            route += [(low, high), (high, low)]
    return lax.ppermute(block, axis, route)


def combined_all(shard, axis, join):
    gathered = jax.tree.map(
        lambda a, kind: lax.all_gather(a.astype(kind), axis),
        shard,
        jax.tree.map(lambda a: jnp.bfloat16 if a.dtype == jnp.float32 else a.dtype, shard),
    )

    def take(source):
        return jax.tree.map(
            lambda a, own: lax.dynamic_index_in_dim(a, source, 0, False).astype(own.dtype),
            gathered,
            shard,
        )

    return lax.fori_loop(
        1, lax.axis_size(axis), lambda source, state: join(state, take(source)), take(0)
    )


def partial_attend(heads, keys, values, allowed, scale):
    scores = jnp.einsum("rkgd,nkd->rkgn", heads, keys, preferred_element_type=jnp.float32) * scale
    wide_mask = allowed[:, None, None, :]
    scores = jnp.where(wide_mask, scores, -1e30)
    top = jnp.max(scores, axis=-1)
    weights = jnp.where(wide_mask, jnp.exp(scores - top[..., None]), 0.0)
    total = jnp.sum(weights, axis=-1)
    summed = jnp.einsum(
        "rkgn,nkd->rkgd", weights.astype(jnp.bfloat16), values, preferred_element_type=jnp.float32
    )
    return (top, total, summed)


def combine(first, second):
    top = jnp.maximum(first[0], second[0])
    left = jnp.exp(first[0] - top)
    right = jnp.exp(second[0] - top)
    return (
        top,
        first[1] * left + second[1] * right,
        first[2] * left[..., None] + second[2] * right[..., None],
    )


def general_path(
    tokens, norm_gain, w_query, w_key, w_value, w_out, cache_keys, cache_values, seg_ids, block_ids
):
    groups = seg_ids.shape[0]
    rows = seg_ids.shape[1]
    steps = block_ids.shape[1]
    group = lax.axis_index(("req", "kv"))
    tp_index = lax.axis_index("tp")
    head_dim = HD
    gsize = HQ // KVH
    local_heads = w_query.shape[1] // head_dim
    per_kv = min(gsize, local_heads)
    kv_count = local_heads // per_kv
    first_kv = tp_index * local_heads // gsize
    scale = head_dim ** (-0.5)
    blocks_here = cache_keys.shape[0]
    block_len = cache_keys.shape[1]
    blocks_all = blocks_here * groups
    wide = tokens[0].astype(jnp.float32)
    normed = (
        wide
        * lax.rsqrt(jnp.mean(wide * wide, axis=-1, keepdims=True) + EPS)
        * norm_gain.astype(jnp.float32)
    ).astype(jnp.bfloat16)
    whole = lax.all_gather(normed, "tp", axis=0, tiled=True)
    pieces = (
        lax.all_gather(w_query, ("req", "kv"), axis=0, tiled=True),
        lax.all_gather(w_key, ("req", "kv"), axis=0, tiled=True),
        lax.all_gather(w_value, ("req", "kv"), axis=0, tiled=True),
    )
    query_acc, key_acc, value_acc = tuple(
        (jnp.dot(whole, piece, preferred_element_type=jnp.float32) for piece in pieces)
    )
    queries = query_acc.astype(jnp.bfloat16)
    span = max(1, gsize // local_heads)
    stacked = jnp.stack((key_acc.astype(jnp.bfloat16), value_acc.astype(jnp.bfloat16)))
    for bit in range(span.bit_length() - 1):
        partner = swapped(stacked, "tp", bit)
        upper = tp_index // (1 << bit) % 2 == 1
        stacked = jnp.where(
            upper, jnp.concatenate((partner, stacked), 2), jnp.concatenate((stacked, partner), 2)
        )
    own_keys = stacked[0].reshape(rows, kv_count, head_dim)
    own_values = stacked[1].reshape(rows, kv_count, head_dim)
    heads = queries.reshape(rows, kv_count, per_kv, head_dim)
    member = jnp.any(
        block_ids[..., None] == jnp.arange(blocks_all, dtype=jnp.int32), axis=-2
    ).astype(jnp.float32)
    onehot = (seg_ids[..., None] == jnp.arange(steps, dtype=jnp.int32)).astype(jnp.float32)
    block_mask = jnp.einsum("grs,gsb->grb", onehot, member) > 0.5
    seg_here = lax.dynamic_index_in_dim(seg_ids, group, 0, keepdims=False)
    places = jnp.arange(rows, dtype=jnp.int32)
    own_mask = (seg_here[:, None] == seg_here[None, :]) & (places[:, None] >= places[None, :])
    own_part = partial_attend(heads, own_keys, own_values, own_mask, scale)
    gathered = lax.all_gather(queries[None], ("req", "kv"), axis=0, tiled=True)
    all_heads = gathered.reshape(groups * rows, kv_count, per_kv, head_dim)
    local_keys = lax.dynamic_slice_in_dim(
        cache_keys, first_kv * head_dim, kv_count * head_dim, 2
    ).reshape(blocks_here * block_len, kv_count, head_dim)
    local_values = lax.dynamic_slice_in_dim(
        cache_values, first_kv * head_dim, kv_count * head_dim, 2
    ).reshape(blocks_here * block_len, kv_count, head_dim)
    local_blocks = lax.dynamic_slice_in_dim(
        block_mask, group * blocks_here, blocks_here, 2
    ).reshape(groups * rows, blocks_here)
    local_mask = jnp.repeat(local_blocks, block_len, axis=1)
    cache_part = partial_attend(all_heads, local_keys, local_values, local_mask, scale)
    merged = combined_all(cache_part, ("req", "kv"), combine)
    mine = tuple((lax.dynamic_slice_in_dim(item, group * rows, rows, 0) for item in merged))
    top, total, summed = combine(mine, own_part)
    attended = (
        (summed / total[..., None]).astype(jnp.bfloat16).reshape(rows, local_heads * head_dim)
    )
    out_full = lax.all_gather(w_out, ("req", "kv"), axis=1, tiled=True)
    branch = lax.psum_scatter(
        jnp.dot(attended, out_full, preferred_element_type=jnp.float32).astype(jnp.bfloat16),
        "tp",
        scatter_dimension=0,
        tiled=True,
    )
    return branch[None]


SWAP = [(0, 1), (1, 0)]
MASKED = -1e30
MIB = 2**20


def tp_ring(count):
    return list(range(0, count, 2)) + list(range(1, count, 2))[::-1]


def after(value, *gates):
    if not gates:
        return value
    return lax.optimization_barrier((value, gates))[0]


def norm_kernel(place_ref, x_ref, gain_ref, keep_ref, give_ref, far_ref, cross_ref):
    wide = x_ref[0].astype(jnp.float32)
    factor = lax.rsqrt(jnp.mean(wide * wide, axis=1, keepdims=True) + EPS)
    width = keep_ref.shape[1]
    req, kv = place_ref[0], place_ref[1]
    to = (2 * req + kv, 2 * req + 1 - kv, 2 - 2 * req + kv, 3 - 2 * req - kv)
    for quarter, ref in zip(to, (keep_ref, give_ref, far_ref, cross_ref)):
        at = pl.multiple_of(quarter * width, width)
        part = x_ref[0, :, pl.ds(at, width)].astype(jnp.float32)
        gain = gain_ref[:, pl.ds(at, width)].astype(jnp.float32)
        ref[...] = (part * factor * gain).astype(ref.dtype)


def norm(place, tokens, gain):
    rows, depth = tokens.shape[1:]
    whole = pl.BlockSpec(memory_space=pltpu.VMEM)
    quarter = jax.ShapeDtypeStruct((rows, depth // 4), jnp.bfloat16)
    return pl.pallas_call(
        norm_kernel,
        in_specs=[pl.BlockSpec(memory_space=pltpu.SMEM), whole, whole],
        out_specs=[whole] * 4,
        out_shape=[quarter] * 4,
        compiler_params=pltpu.CompilerParams(vmem_limit_bytes=4 * MIB),
        name="norm",
    )(place, tokens, gain.reshape(1, depth))


def load_kernel(count, *refs):
    copies = [
        pltpu.make_async_copy(source, to, refs[-1].at[number])
        for number, (source, to) in enumerate(zip(refs[:count], refs[count:]))
    ]
    for copy in copies:
        copy.start()
    for copy in copies:
        copy.wait()


def load(limit, *arrays):
    count = len(arrays)
    return pl.pallas_call(
        functools.partial(load_kernel, count),
        in_specs=[pl.BlockSpec(memory_space=pl.ANY)] * count,
        out_specs=[pl.BlockSpec(memory_space=pltpu.VMEM)] * count,
        out_shape=[pltpu.VMEM(a.shape, a.dtype) for a in arrays],
        scratch_shapes=[pltpu.SemaphoreType.DMA((count,))],
        compiler_params=pltpu.CompilerParams(vmem_limit_bytes=limit * MIB),
        name="load",
    )(*arrays)


def heads_kernel(place_ref, k_ref, v_ref, mine_ref, give_ref, sems):
    head_dim = mine_ref.shape[-1]
    kv, tp = place_ref[1], place_ref[2]
    copies = []
    for number, (out, core) in enumerate(((mine_ref, kv), (give_ref, 1 - kv))):
        at = pl.multiple_of((2 * tp + core) * head_dim, head_dim)
        for which, ref in enumerate((k_ref, v_ref)):
            copies.append(
                pltpu.make_async_copy(
                    ref.at[:, :, pl.ds(at, head_dim)], out.at[which], sems.at[2 * number + which]
                )
            )
    for copy in copies:
        copy.start()
    for copy in copies:
        copy.wait()


def cached_heads(place, keys, values):
    blocks, length = keys.shape[:2]
    out = jax.ShapeDtypeStruct((2, blocks, length, HD), keys.dtype)
    return pl.pallas_call(
        heads_kernel,
        in_specs=[pl.BlockSpec(memory_space=pltpu.SMEM)]
        + [pl.BlockSpec(memory_space=pl.ANY)] * 2,
        out_specs=[pl.BlockSpec(memory_space=pltpu.VMEM)] * 2,
        out_shape=[out] * 2,
        scratch_shapes=[pltpu.SemaphoreType.DMA((4,))],
        compiler_params=pltpu.CompilerParams(vmem_limit_bytes=4 * MIB),
        name="cached_heads",
    )(place, keys, values)


def collect_kernel(place_ref, *refs):
    terms, out_ref = refs[:-1], refs[-1]
    width = terms[0].shape[1]
    req, kv = place_ref[0], place_ref[1]
    of = (2 * req + kv, 2 * req + 1 - kv, 2 - 2 * req + kv, 3 - 2 * req - kv)
    pairs = (terms[:1], terms[1:2], terms[2:4], terms[4:])
    for quarter, pair in zip(of, pairs):
        total = sum(term[...].astype(jnp.float32) for term in pair)
        at = pl.ds(pl.multiple_of(quarter * width, width), width)
        out_ref[0, :, at] = total.astype(out_ref.dtype)


def collect(place, mine, theirs, same, cross):
    rows, columns = mine.shape
    whole = pl.BlockSpec(memory_space=pltpu.VMEM)
    return pl.pallas_call(
        collect_kernel,
        in_specs=[pl.BlockSpec(memory_space=pltpu.SMEM)] + [whole] * 6,
        out_specs=whole,
        out_shape=jax.ShapeDtypeStruct((1, rows, 4 * columns), mine.dtype),
        compiler_params=pltpu.CompilerParams(vmem_limit_bytes=4 * MIB),
        name="collect",
    )(place, mine, theirs, *same, *cross)


def project_kernel(flips, place_ref, *refs):
    outputs = len(flips)
    pieces = refs[: -3 - outputs]
    q_ref, k_ref, v_ref = refs[-3 - outputs : -outputs]
    outs = refs[-outputs:]
    x = jnp.concatenate([piece[...] for piece in pieces], axis=0)
    head_dim = k_ref.shape[1] // 2
    width = 256
    base = q_ref.shape[1] // 2
    for number, out in enumerate(outs):
        kv = place_ref[1]
        half = 1 - kv if flips[number] else kv
        for t in range(base // width):
            at = pl.multiple_of(half * base + t * width, width)
            product = jnp.dot(x, q_ref[:, pl.ds(at, width)], preferred_element_type=jnp.float32)
            out[:, t * width : (t + 1) * width] = product.astype(out.dtype)
        at = pl.ds(pl.multiple_of(half * head_dim, head_dim), head_dim)
        both = jnp.concatenate((k_ref[:, at], v_ref[:, at]), axis=1)
        product = jnp.dot(x, both, preferred_element_type=jnp.float32)
        out[:, base:] = product.astype(out.dtype)


def project(place, pieces, weights, flips, kinds):
    rows = sum(piece.shape[0] for piece in pieces)
    total = sum(w.shape[1] for w in weights) // 2
    whole = pl.BlockSpec(memory_space=pltpu.VMEM)
    return pl.pallas_call(
        functools.partial(project_kernel, flips),
        in_specs=[pl.BlockSpec(memory_space=pltpu.SMEM)] + [whole] * (len(pieces) + 3),
        out_specs=[whole] * len(kinds),
        out_shape=[jax.ShapeDtypeStruct((rows, total), kind) for kind in kinds],
        compiler_params=pltpu.CompilerParams(vmem_limit_bytes=6 * MIB),
        name="project",
    )(place, *pieces, *weights)


def out_kernel(place_ref, own_ref, other_ref, w_ref, *outs):
    depth = own_ref.shape[1]
    part = own_ref.shape[0] // len(outs)
    mine = place_ref[1]
    at = pl.multiple_of(mine * depth, depth)
    off = pl.multiple_of((1 - mine) * depth, depth)
    own, other = own_ref[...], other_ref[...]
    width = 256
    for t in range(w_ref.shape[1] // width):
        columns = slice(t * width, (t + 1) * width)
        product = jnp.dot(
            own, w_ref[pl.ds(at, depth), columns], preferred_element_type=jnp.float32
        )
        product += jnp.dot(
            other, w_ref[pl.ds(off, depth), columns], preferred_element_type=jnp.float32
        )
        product = product.astype(outs[0].dtype)
        for j, out in enumerate(outs):
            out[:, columns] = product[j * part : (j + 1) * part]


def out_project(place, own, other, w_out, pieces):
    rows = own.shape[0]
    columns = w_out.shape[1]
    whole = pl.BlockSpec(memory_space=pltpu.VMEM)
    return pl.pallas_call(
        out_kernel,
        in_specs=[pl.BlockSpec(memory_space=pltpu.SMEM)] + [whole] * 3,
        out_specs=[whole] * pieces,
        out_shape=[jax.ShapeDtypeStruct((rows // pieces, columns), jnp.bfloat16)] * pieces,
        compiler_params=pltpu.CompilerParams(vmem_limit_bytes=6 * MIB),
        name="out_project",
    )(place, own, other, w_out)


def attend_kernel(wanted, order, parts, place_ref, ids_ref, seg_ref, *refs):
    keep_refs, come_refs = refs[:parts], refs[parts:-3]
    chip_ref, away_ref, out_ref = refs[-3:]
    req, kv, tp = place_ref[0], place_ref[1], place_ref[2]
    groups = 2
    steps = ids_ref.shape[1]
    total_cols = keep_refs[0].shape[1]
    rows = sum(ref.shape[0] for ref in keep_refs) // groups
    part = out_ref.shape[0] // (groups * len(wanted))
    pieces = rows // part
    some = part * len(wanted)
    head_dim = chip_ref.shape[-1]
    blocks, length = chip_ref.shape[2:4]
    heads = total_cols // head_dim - 2
    q_cols = heads * head_dim
    scale = head_dim**-0.5 * math.log2(math.e)
    stack = min(heads, max(1, 256 // some))
    chain = CHAIN_BLOCKS * length

    def looked_up(index, options):
        result = jnp.int32(options[0])
        for number, option in enumerate(options[1:], 1):
            result = jnp.where(index == number, jnp.int32(option), result)
        return result

    spot = looked_up(tp, [order.index(i) for i in range(pieces)])
    source = [looked_up(lax.rem(spot - j + pieces, pieces), order) for j in range(pieces)]

    def branch(block, which):
        device = block // blocks
        near = device // 2 == req
        core = jnp.where(lax.rem(device, 2) == kv, 0, 1)
        at = lax.rem(block, blocks)
        here = chip_ref[core, which, pl.ds(at, CHAIN_BLOCKS)]
        there = away_ref[core, which, pl.ds(at, CHAIN_BLOCKS)]
        return jnp.where(near, here, there).reshape(chain, head_dim)

    def position(index, sources):
        piece = index // part
        start = jnp.full(index.shape, source[sources[0]], jnp.int32)
        for j in range(1, len(sources)):
            start = jnp.where(piece == j, source[sources[j]], start)
        return start * part + index % part

    row_pos = position(lax.broadcasted_iota(jnp.int32, (some, rows), 0), wanted)
    across = lax.broadcasted_iota(jnp.int32, (some, rows), 1)
    col_pos = position(across, range(pieces))
    keep = jnp.concatenate([ref[...] for ref in keep_refs], axis=0)
    come = jnp.concatenate([ref[...] for ref in come_refs], axis=0)
    whole = (keep + come.astype(jnp.float32)).astype(jnp.bfloat16)

    def own_rows(g, j, columns):
        at = (j * groups + g) * part
        return whole[at : at + part, columns]

    for g in range(groups):
        group = 2 * req + g
        segments = seg_ref[pl.ds(group, 1), :]
        root = jnp.int32(0)
        keys, values = [branch(root, 0)], [branch(root, 1)]
        bias = []
        same = None
        low = jnp.int32(0)
        for s in range(steps):
            first = ids_ref[group, s, ROOT_BLOCKS]
            count = jnp.int32(0)
            for slot in range(CHAIN_BLOCKS):
                count += jnp.where(ids_ref[group, s, ROOT_BLOCKS + slot] >= 0, length, 0)
            high = jnp.sum((segments <= s).astype(jnp.int32))
            keys.append(branch(first, 0))
            values.append(branch(first, 1))
            row_in = (row_pos >= low) & (row_pos < high)
            col_in = (col_pos >= low) & (col_pos < high)
            both = row_in & col_in
            same = both if same is None else same | both
            for piece in range(chain // rows):
                allowed = row_in & (across + piece * rows < count)
                bias.append(jnp.where(allowed, 0.0, MASKED))
            low = high
        for j in range(pieces):
            keys.append(own_rows(g, j, slice(q_cols, q_cols + head_dim)))
            values.append(own_rows(g, j, slice(q_cols + head_dim, None)))
        bias.append(jnp.where(same & (col_pos <= row_pos), 0.0, MASKED))
        keys = jnp.concatenate(keys, axis=0)
        values = jnp.concatenate(values, axis=0)
        bias = jnp.concatenate(bias, axis=1)
        bias = jnp.concatenate([bias] * stack, axis=0)
        for low_head in range(0, heads, stack):
            query = jnp.concatenate(
                [
                    own_rows(g, j, slice(h * head_dim, (h + 1) * head_dim))
                    for h in range(low_head, low_head + stack)
                    for j in wanted
                ],
                axis=0,
            )
            scores = lax.dot_general(
                query, keys, (((1,), (1,)), ((), ())), preferred_element_type=jnp.float32
            )
            scores = scores * scale
            scores = jnp.concatenate((scores[:, :chain], scores[:, chain:] + bias), axis=1)
            top = jnp.max(scores, axis=1, keepdims=True)
            weights = jnp.exp2(scores - top)
            total = jnp.sum(weights, axis=1, keepdims=True)
            summed = jnp.dot(
                weights.astype(jnp.bfloat16), values, preferred_element_type=jnp.float32
            )
            result = (summed / total).astype(out_ref.dtype)
            for n in range(stack):
                columns = slice((low_head + n) * head_dim, (low_head + n + 1) * head_dim)
                for number in range(len(wanted)):
                    of, to = n * some + number * part, (number * groups + g) * part
                    out_ref[to : to + part, columns] = result[of : of + part]


def attend(wanted, order, place, ids, segments, keep, come, chip, away, part):
    rows = 2 * len(wanted) * part
    whole = pl.BlockSpec(memory_space=pltpu.VMEM)
    scalars = pl.BlockSpec(memory_space=pltpu.SMEM)
    return pl.pallas_call(
        functools.partial(attend_kernel, wanted, order, len(keep)),
        in_specs=[scalars] * 2 + [whole] * (len(keep) + len(come) + 3),
        out_specs=whole,
        out_shape=jax.ShapeDtypeStruct((rows, keep[0].shape[1] - 2 * HD), jnp.bfloat16),
        compiler_params=pltpu.CompilerParams(vmem_limit_bytes=10 * MIB),
        name="attend",
    )(place, ids, segments, *keep, *come, chip, away)


ROOT_BLOCKS = 4
CHAIN_BLOCKS = 4


def on_device(
    tokens, norm_gain, w_query, w_key, w_value, w_out, cache_keys, cache_values, seg_ids, block_ids
):
    req, kv, tp = lax.axis_index("req"), lax.axis_index("kv"), lax.axis_index("tp")
    part = tokens.shape[1]
    count = lax.axis_size("tp")
    order = tp_ring(count)
    forward = [(order[i], order[(i + 1) % count]) for i in range(count)]
    place = jnp.stack((req, kv, tp)).astype(jnp.int32)

    def swap_req(x):
        return lax.ppermute(x, "req", SWAP)

    def swap_kv(x):
        return lax.ppermute(x, "kv", SWAP)

    def swap_both(x):
        return lax.ppermute(x, ("req", "kv"), [(i, 3 - i) for i in range(4)])

    def onward(x):
        return lax.ppermute(x, "tp", forward)

    def slanted(same, cross):
        axes = ("tp", "req", "kv")
        return [
            lax.ppermute(
                x,
                axes,
                [
                    (4 * low + 2 * r + c, 4 * high + 2 * (1 - r) + (c ^ flip))
                    for low, high in forward
                    for r in range(2)
                    for c in range(2)
                ],
            )
            for flip, x in enumerate((same, cross))
        ]

    first = kv == 0

    def merged(mine, theirs):
        return jnp.where(
            first, jnp.concatenate((mine, theirs)), jnp.concatenate((theirs, mine))
        )

    def shared(rows):
        low, high = rows[:part], rows[part:]
        return jnp.where(first, low, high), jnp.where(first, high, low)

    kept, give, far_same, far_cross = norm(place, tokens, norm_gain)
    near = merged(kept, swap_kv(give))
    far = merged(swap_req(far_same), swap_both(far_cross))

    kinds = (jnp.bfloat16, jnp.float32)

    def summed(sent, kept, kind):
        return (kept + swap_kv(sent).astype(jnp.float32)).astype(kind)

    near_pieces, far_pieces = [near, onward(near)], [far]
    weights = load(46, *after((w_query, w_key, w_value), near))
    far_pieces.append(onward(after(far, weights)))
    mine, give = cached_heads(place, *after((cache_keys, cache_values), weights))
    chip = jnp.stack((mine, swap_kv(give)))
    away = swap_req(chip)
    far_first = project(place, far_pieces, weights, (True, False), kinds)
    for step in range(1, count - 1):
        piece = near_pieces[step]
        near_pieces.append(onward(after(piece, far_first) if step == count - 2 else piece))
        far_pieces.append(onward(far_pieces[step]))
    first_terms = summed(*far_first, jnp.bfloat16)

    near_terms = project(place, near_pieces, weights, (True, False), kinds)
    keep = (summed(*near_terms, jnp.float32),)
    pieces = after(far_pieces[2:], near_terms, away)
    sent = project(place, pieces, weights, (True,), kinds[:1])
    kept = project(place, pieces, weights, (False,), kinds[1:])
    last_terms = summed(*sent, *kept, jnp.bfloat16)
    come = (swap_req(first_terms), swap_req(last_terms))
    w_out = load(38, *after((w_out,), last_terms))[0]

    middle = count // 2
    halves = (tuple(range(1, middle + 1)), tuple(j % count for j in range(middle + 1, count + 1)))
    near_sum, far_sum = {}, {}

    def attended(wanted, *gates):
        inputs = after(keep, *gates)
        return attend(
            wanted, order, place, block_ids, seg_ids, inputs, come, chip, away, part
        )

    def projected(sums, wanted, own, other):
        sums |= zip(wanted, out_project(place, own, other, w_out, len(wanted)))

    def plus(running, term):
        return (running.astype(jnp.float32) + term.astype(jnp.float32)).astype(jnp.bfloat16)

    rows = attended(halves[0], w_out)
    rows_far = swap_req(rows)
    projected(near_sum, halves[0], rows, swap_kv(rows))
    near_run = near_one = onward(near_sum[1])
    last = attended(halves[1], near_sum[1])
    last_far = swap_req(last)
    rows_far = after(rows_far, last)
    rows_far = after((rows_far, swap_kv(rows_far)), last)
    projected(far_sum, halves[0], *rows_far)
    far_run = onward(far_sum[1])
    projected(near_sum, halves[1], last, swap_kv(last))
    last_far = after(last_far, near_one)
    projected(far_sum, halves[1], last_far, swap_kv(last_far))

    terms = shared(after(far_sum[0], far_run))
    beside = (swap_req(terms[0]), swap_both(terms[1]))
    for j in range(2, count):
        near_term = plus(near_run, near_sum[j])
        near_run = onward(after(near_term, terms) if j == count - 1 else near_term)
        if j < count - 1:
            far_run = onward(plus(far_run, far_sum[j]))
    ends = slanted(*shared(plus(far_run, far_sum[count - 1])))
    mine, give = shared(plus(near_run, near_sum[0]))
    return collect(place, mine, swap_kv(give), *zip(ends, beside))


def fits(shape):
    local_kv = KVH // shape["tp"]
    return shape["req"] == 2 and shape["kv"] == 2 and shape["tp"] > 1 and local_kv == 2


def solution(mesh):
    placed = (
        P(("grp", "req", "kv"), "tp", None),
        P(),
        P(("req", "kv"), "tp"),
        P(("req", "kv"), "tp"),
        P(("req", "kv"), "tp"),
        P("tp", ("req", "kv")),
        P(("grp", "req", "kv"), None, None),
        P(("grp", "req", "kv"), None, None),
        P("grp", None),
        P("grp", None, None),
    )
    return jax.shard_map(
        on_device if fits(mesh.shape) else general_path,
        mesh=mesh,
        in_specs=placed,
        out_specs=P(("grp", "req", "kv"), "tp", None),
        check_vma=False,
    )
```
